32 devices in a mesh: dp: 16 (over z, y, x), tensor: 2 (over core).
Axes of the slice: x: 2, y: 2, z: 4, core: 2. Of those that a mesh axis runs over, the one named last changes fastest.
Arguments:
- normed: bfloat16 [1024, 1280], P('dp'), may hold values from -6 to 6
- residual_in: bfloat16 [1024, 1280], P('dp'), may hold values from -6 to 6
- w_up: bfloat16 [1280, 5120], P('dp', 'tensor'), may hold values from -0.15625 to 0.15625
- w_down: bfloat16 [5120, 1280], P('tensor', 'dp'), may hold values from -0.15625 to 0.15625
- final_gain: float32 [1280], replicated, may hold values from 0.1 to 1.9
- head_cols: bfloat16 [1280, 16], replicated, may hold values from -4 to 4
- sub_inputs: int32 [2048], P('tensor'), may hold values from 0 to 1279
- sub_hidden: int32 [2048], P('tensor'), may hold values from 0 to 5119, as said below
- panels: bfloat16 [2, 256, 2048], P(None, 'dp', 'tensor'), may hold values from -0.1001 to 0.1001, as said below
- inverses: bfloat16 [2, 256, 256], replicated, may hold values from -0.1001 to 2, as said below
Outputs:
- whitened: bfloat16 [1024, 16, 2048], P('dp', None, 'tensor')
The draws below stay inside these ranges and needn't reach their ends.
Inputs may be any that keep to these rules, and one draw needn't show every extreme that they name: `sub_hidden`: window rows t * 1024 to (t + 1) * 1024 - 1 name hidden units t * 2560 to (t + 1) * 2560 - 1. `panels`: entry [q, c, r] is zero for r < (q + 1) * 256. `inverses`: each block is lower triangular with a positive diagonal.
All inputs are finite; a program needn't handle non-finite values.
Results may differ from the reference program's by a relative error of at most 0.0069.
Values may be sent and summed in bfloat16 or wider, within the bound.
A program may use at most 64 MiB of HBM per device.

```python
import math
import jax
import jax.numpy as jnp
from jax import lax

D = 1280
FF = 5120
LOGITS = 16
PANEL = 256
IMG_DEV = 64
ROWS_T = 1024
FF_T = 2560
WROWS = 2048
IMGS = 1024


def draw_sub_hidden(key, part):
    row_ids = jnp.arange(WROWS, dtype=jnp.int32)
    owner = row_ids // ROWS_T
    within = row_ids % ROWS_T
    picked = jax.random.randint(key, (WROWS,), 0, FF_T, dtype=jnp.int32)
    picked = jnp.where(within == 0, 0, jnp.where(within == 1, FF_T - 1, picked))
    return (owner * FF_T + picked).astype(jnp.int32)


def draw_panels(key, part):
    key_vals = jax.random.fold_in(jax.random.fold_in(key, 11), 0)
    values = jax.random.uniform(key_vals, (2, PANEL, WROWS), jnp.float32, -0.1, 0.1)
    row_ids = jnp.arange(WROWS, dtype=jnp.int32)[None, None, :]
    which = jnp.arange(2, dtype=jnp.int32)[:, None, None]
    values = jnp.where(row_ids >= (which + 1) * PANEL, values, 0.0)
    return values.astype(jnp.bfloat16)


def draw_inverses(key, part):
    key_diag, key_off = jax.random.split(jax.random.fold_in(key, 23))
    diag_vals = jnp.exp(jax.random.uniform(key_diag, (2, PANEL), jnp.float32, math.log(0.5), math.log(2.0)))
    off_vals = jax.random.uniform(key_off, (2, PANEL, PANEL), jnp.float32, -0.1, 0.1)
    row_ids = jnp.arange(PANEL, dtype=jnp.int32)[:, None]
    col_ids = jnp.arange(PANEL, dtype=jnp.int32)[None, :]
    lower = (row_ids > col_ids)[None, :, :]
    diagonal = (row_ids == col_ids)[None, :, :]
    values = jnp.where(lower, off_vals, 0.0) + jnp.where(diagonal, diag_vals[:, :, None], 0.0)
    return values.astype(jnp.bfloat16)


def place_ends(values, own_key, least, largest):
    longest = values.shape.index(max(values.shape))
    spots = []
    for shift in (0, 1):
        where = [jax.random.randint(jax.random.fold_in(own_key, axis), (), 0, length) for axis, length in enumerate(values.shape)]
        where[longest] = (where[longest] + shift) % values.shape[longest]
        spots.append(tuple(where))
    return values.at[spots[0]].set(least).at[spots[1]].set(largest)


def block_scale(stream_key, dims, shards, low, largest):
    def one(axis_at, blocks):
        draws = jax.random.uniform(jax.random.fold_in(jax.random.fold_in(stream_key, 6), axis_at), (blocks,), jnp.float32, low / len(shards), largest / len(shards))
        return jnp.repeat(jnp.exp(draws), dims[axis_at] // blocks).reshape((-1,) + (1,) * (len(dims) - axis_at - 1))

    factor_of = one(*shards[0])
    for cut in shards[1:]:
        factor_of = factor_of * one(*cut)
    return factor_of


def noise(rng, shape, spread, limit, cuts=(), held_as=jnp.bfloat16):
    loudness = block_scale(rng, shape, cuts, -0.22, 0.18) if cuts else 1.0
    values = jax.random.normal(rng, shape, jnp.float32) * spread * loudness
    return jnp.minimum(jnp.maximum(values, -limit), limit).astype(held_as)


def setup_inputs(seed: int = 0) -> dict:
    splits = jax.random.split(jax.random.key(seed), 11)
    return {
        "normed": noise(splits[0], (IMGS, D), 1.0, 6.0, ((0, 16),)),
        "residual_in": noise(splits[1], (IMGS, D), 1.0, 6.0, ((0, 16),)),
        "w_up": noise(splits[2], (D, FF), D ** -0.5, 0.15625, ((0, 16), (1, 2))),
        "w_down": noise(splits[3], (FF, D), D ** -0.5, 0.15625, ((0, 2), (1, 16))),
        "final_gain": jnp.clip(1.0 + 0.18 * jax.random.normal(splits[4], (D,), jnp.float32), 0.1, 1.9),
        "head_cols": noise(splits[5], (D, LOGITS), 1.0, 4.0),
        "sub_inputs": place_ends(jax.random.randint(splits[6], (WROWS,), 0, D), jax.random.fold_in(splits[6], 1), 0, D - 1).astype(jnp.int32),
        "sub_hidden": draw_sub_hidden(jax.random.fold_in(splits[10], 71), 0),
        "panels": draw_panels(jax.random.fold_in(splits[10], 71), 0),
        "inverses": draw_inverses(jax.random.fold_in(splits[10], 71), 0),
    }


def gelu_parts(values):
    normal_cdf = 0.5 * (1.0 + jax.scipy.special.erf(values * 0.7071067811865476))
    slope = normal_cdf + values * jnp.exp(-0.5 * values * values) * 0.3989422804014327
    return (values * normal_cdf, slope)

def logit_adjoint(block_result, final_gain, head_cols):
    mean_x = lax.optimization_barrier(jnp.mean(block_result, axis=1, keepdims=True))
    centred_rows = block_result - mean_x
    inverse_deviation = lax.rsqrt(lax.optimization_barrier(jnp.mean(centred_rows * centred_rows, axis=1, keepdims=True)) + 1e-06)
    normalized_input = centred_rows * inverse_deviation
    head_scaled_rows = final_gain[:, None] * head_cols.astype(jnp.float32)
    head_average = lax.optimization_barrier(jnp.mean(head_scaled_rows, axis=0))
    project_rows = jnp.dot(normalized_input, head_scaled_rows, precision=lax.Precision.HIGHEST) / block_result.shape[1]
    return inverse_deviation[:, :, None] * (head_scaled_rows.T[None, :, :] - head_average[None, :, None] - normalized_input[:, None, :] * project_rows[:, :, None])

def apply_inverse(block, inverse):
    return lax.dot_general(block, inverse, (((1,), (1,)), ((), ())), preferred_element_type=jnp.float32)

def reference(normed, residual_in, w_up, w_down, final_gain, head_cols, sub_inputs, sub_hidden, panels, inverses):

    def one_block(first_row):
        inputs = lax.dynamic_slice_in_dim(normed, first_row, IMG_DEV, 0)
        before = lax.dynamic_slice_in_dim(residual_in, first_row, IMG_DEV, 0)
        up_pre = jnp.dot(inputs, w_up, preferred_element_type=jnp.float32)
        activ, slope = gelu_parts(up_pre)
        hidden = activ.astype(jnp.bfloat16)
        block_result = before.astype(jnp.float32) + jnp.dot(hidden, w_down, preferred_element_type=jnp.float32)
        adjoint = logit_adjoint(block_result, final_gain, head_cols).astype(jnp.bfloat16)
        back = lax.dot_general(adjoint.reshape(IMG_DEV * LOGITS, D), w_down, (((1,), (1,)), ((), ())), preferred_element_type=jnp.float32)
        delta = back.reshape(IMG_DEV, LOGITS, FF) * slope[:, None, :]
        picked = jnp.take(inputs, sub_inputs, axis=1).astype(jnp.float32)
        jac = (picked[:, None, :] * jnp.take(delta, sub_hidden, axis=2)).astype(jnp.bfloat16)
        jac = jac.reshape(IMG_DEV * LOGITS, WROWS)
        first = apply_inverse(jac[:, :PANEL], inverses[0]).astype(jnp.bfloat16)
        carry = jnp.dot(first, panels[0], preferred_element_type=jnp.float32)
        second_in = (jac[:, PANEL:2 * PANEL].astype(jnp.float32) - carry[:, PANEL:2 * PANEL]).astype(jnp.bfloat16)
        second = apply_inverse(second_in, inverses[1]).astype(jnp.bfloat16)
        update = carry + jnp.dot(second, panels[1], preferred_element_type=jnp.float32)
        below = (jac.astype(jnp.float32) - update).astype(jnp.bfloat16)
        result = jnp.concatenate([first, second, below[:, 2 * PANEL:]], axis=1)
        return result.reshape(IMG_DEV, LOGITS, WROWS)
    starts = jnp.arange(IMGS // IMG_DEV, dtype=jnp.int32) * IMG_DEV
    return lax.map(one_block, starts).reshape(IMGS, LOGITS, WROWS)
```

```python
import functools

import jax
import jax.numpy as jnp
from jax import lax
from jax.experimental import pallas as pl
from jax.experimental.pallas import tpu as pltpu
from jax.sharding import PartitionSpec as P

MESH = pl.DeviceIdType.MESH
GROUP = 4
F32 = jnp.float32
BF16 = jnp.bfloat16


def gelu_parts(values):
    normal_cdf = 0.5 * (1.0 + lax.erf(values * 0.7071067811865476))
    slope = normal_cdf + values * jnp.exp(-0.5 * values * values) * 0.3989422804014327
    return (values * normal_cdf, slope)


def normalize(block_result):
    mean_x = jnp.mean(block_result, axis=1, keepdims=True)
    centred = block_result - mean_x
    inv_std = lax.rsqrt(jnp.mean(centred * centred, axis=1, keepdims=True) + 1e-06)
    return centred * inv_std, inv_std


def front_kernel(
    planes,
    pairs,
    normed_ref, resid_ref, wup_ref, wdt_ref, head_ref,
    side_ref, back_ref, xhat_ref, istd_ref,
    nall, wu, wd, part, parts_in, pair_out, pair_in, xown, xall,
    side_src, side_in, back_src, back_in,
    local_sem, flat_send, flat_recv, up_send, up_recv, dn_send, dn_recv, pair_send, pair_recv,
):
    d = lax.axis_index("dp")
    t = lax.axis_index("tensor")
    z = d // GROUP
    p = lax.rem(d, GROUP)
    images, width = normed_ref.shape
    cols = wu.shape[3]
    logits = head_ref.shape[0] // 2
    last = planes - 1
    others = range(1, GROUP)

    barrier = pltpu.get_barrier_semaphore()
    for o in others:
        pl.semaphore_signal(barrier, inc=1, device_id=(z * GROUP + (p ^ o), t), device_id_type=MESH)
    pl.semaphore_signal(barrier, inc=1, device_id=(d, 1 - t), device_id_type=MESH)

    @pl.when(z > 0)
    def _():
        pl.semaphore_signal(barrier, inc=1, device_id=(d - GROUP, t), device_id_type=MESH)

    @pl.when(z < last)
    def _():
        pl.semaphore_signal(barrier, inc=1, device_id=(d + GROUP, t), device_id_type=MESH)

    pl.semaphore_wait(barrier, GROUP + jnp.where(z > 0, 1, 0) + jnp.where(z < last, 1, 0))

    def flat(src, dst, kind, o):
        return pltpu.make_async_remote_copy(
            src_ref=src, dst_ref=dst, send_sem=flat_send.at[kind, o], recv_sem=flat_recv.at[kind, o],
            device_id=(z * GROUP + (p ^ o), t), device_id_type=MESH,
        )

    def block(ref, q):
        return ref.at[:, pl.ds(pl.multiple_of(q * cols, 128), cols)]

    sent = []
    own = [
        pltpu.make_async_copy(block(wup_ref, p), wu.at[z, p], local_sem.at[0]),
        pltpu.make_async_copy(block(wdt_ref, p), wd.at[z, p], local_sem.at[1]),
        pltpu.make_async_copy(normed_ref, nall.at[p], local_sem.at[2]),
    ]
    for copy in own:
        copy.start()
    moves = {}
    for kind in (0, 1, 2):
        for o in others:
            if kind == 0:
                copy = flat(block(wup_ref, p ^ o), wu.at[z, p], 0, o)
            elif kind == 1:
                copy = flat(block(wdt_ref, p ^ o), wd.at[z, p], 1, o)
            else:
                copy = flat(normed_ref, nall.at[p], 2, o)
            copy.start()
            moves[kind, o] = copy
            sent.append(copy)

    def hop(buf, w, src, s, step):
        send, recv = (up_send, up_recv) if step > 0 else (dn_send, dn_recv)
        return pltpu.make_async_remote_copy(
            src_ref=buf.at[src], dst_ref=buf.at[src], send_sem=send.at[w, s], recv_sem=recv.at[w, s],
            device_id=(d + step * GROUP, t), device_id_type=MESH,
        )

    def relay(buf, w, s):
        @pl.when(z >= s)
        def _():
            if s > 0:
                hop(buf, w, z - s, s - 1, 1).wait_recv()

            @pl.when(z < last)
            def _():
                hop(buf, w, z - s, s, 1).start()

        @pl.when(z + s <= last)
        def _():
            if s > 0:
                hop(buf, w, z + s, s - 1, -1).wait_recv()

            @pl.when(z > 0)
            def _():
                hop(buf, w, z + s, s, -1).start()

    for w, buf in enumerate((wu, wd)):
        own[w].wait()
        for o in others:
            moves[w, o].wait_recv()
        relay(buf, w, 0)
    own[2].wait()
    for o in others:
        moves[2, o].wait_recv()
    for s in range(1, planes):
        relay(wu, 0, s)

    rows = GROUP * images
    up_pre = jnp.dot(
        nall[...].reshape(rows, width), wu[...].reshape(width, cols), preferred_element_type=F32
    )
    activ, slope = gelu_parts(up_pre)
    hidden = activ.astype(BF16)
    side_src[:, :images, :] = slope.reshape(GROUP, images, cols)

    for s in range(1, planes):
        relay(wd, 1, s)
    down = wd[...].reshape(width, cols)
    partial = lax.dot_general(hidden, down, (((1,), (1,)), ((), ())), preferred_element_type=F32)
    pair_out[...] = partial.reshape(GROUP, images, width)
    part[...] = partial.astype(BF16).reshape(GROUP, images, width)
    for o in others:
        copy = flat(part.at[p ^ o], parts_in.at[o - 1], 3, o)
        copy.start()
        moves[3, o] = copy
        sent.append(copy)
    head_back = jnp.dot(head_ref[...], down, preferred_element_type=F32)
    head_back = head_back[:logits] + head_back[logits:]
    for q in range(GROUP):
        side_src[q, images:, :] = head_back
    total = pair_out[p]
    for o in others:
        moves[3, o].wait_recv()
        total = total + parts_in[o - 1].astype(F32)
    xhat_ref[...] = total
    swap = pltpu.make_async_remote_copy(
        src_ref=xhat_ref, dst_ref=pair_in, send_sem=pair_send, recv_sem=pair_recv,
        device_id=(d, 1 - t), device_id_type=MESH,
    )
    swap.start()
    swap.wait()
    block_out = resid_ref[...].astype(F32) + (xhat_ref[...] + pair_in[...])
    xhat, inv_std = normalize(block_out)
    xown[...] = xhat.astype(BF16)
    for o in others:
        copy = flat(xown, xall.at[p], 4, o)
        copy.start()
        moves[4, o] = copy
        sent.append(copy)
    xall[p] = xown[...]
    xhat_ref[...] = xhat
    istd_ref[...] = jnp.broadcast_to(inv_std, istd_ref.shape)
    for o in others:
        copy = flat(side_src.at[p ^ o], side_in.at[p], 5, o)
        copy.start()
        moves[5, o] = copy
        sent.append(copy)
    side_in[p] = side_src[p]
    for o in others:
        moves[4, o].wait_recv()
    back = jnp.dot(xall[...].reshape(rows, width), down, preferred_element_type=F32)
    back_src[...] = back.reshape(GROUP, images, cols)
    for o in others:
        copy = flat(back_src.at[p ^ o], back_in.at[p], 6, o)
        copy.start()
        moves[6, o] = copy
        sent.append(copy)
    back_in[p] = back_src[p]
    for kind in (5, 6):
        for o in others:
            moves[kind, o].wait_recv()
    for q in range(GROUP):
        side_ref[:, q * cols : (q + 1) * cols] = side_in[q]
        back_ref[:, q * cols : (q + 1) * cols] = back_in[q]
    for copy in sent:
        copy.wait_send()
    for w, buf in enumerate((wu, wd)):
        for s in range(planes):
            @pl.when((z >= s) & (z < last))
            def _():
                hop(buf, w, z - s, s, 1).wait_send()

            @pl.when((z + s <= last) & (z > 0))
            def _():
                hop(buf, w, z + s, s, -1).wait_send()


def fused_front(normed, residual_in, w_up, w_down, head_pair, members):
    images, width = normed.shape
    depth, hidden_dev = w_up.shape
    logits = head_pair.shape[0] // 2
    planes = members // GROUP
    cols = hidden_dev // GROUP
    side = images + logits
    dma = pltpu.SemaphoreType.DMA
    vmem = pl.BlockSpec(memory_space=pltpu.VMEM)
    return pl.pallas_call(
        functools.partial(front_kernel, planes, 2),
        out_shape=(
            jax.ShapeDtypeStruct((side, hidden_dev), F32),
            jax.ShapeDtypeStruct((images, hidden_dev), F32),
            jax.ShapeDtypeStruct((images, width), F32),
            jax.ShapeDtypeStruct((images, 128), F32),
        ),
        in_specs=[vmem] * 5,
        out_specs=(vmem,) * 4,
        scratch_shapes=[
            pltpu.VMEM((GROUP, images, width), BF16),
            pltpu.VMEM((planes, GROUP, depth, cols), BF16),
            pltpu.VMEM((planes, GROUP, depth, cols), BF16),
            pltpu.VMEM((GROUP, images, width), BF16),
            pltpu.VMEM((GROUP - 1, images, width), BF16),
            pltpu.VMEM((GROUP, images, width), F32),
            pltpu.VMEM((images, width), F32),
            pltpu.VMEM((images, width), BF16),
            pltpu.VMEM((GROUP, images, width), BF16),
            pltpu.VMEM((GROUP, side, cols), F32),
            pltpu.VMEM((GROUP, side, cols), F32),
            pltpu.VMEM((GROUP, images, cols), F32),
            pltpu.VMEM((GROUP, images, cols), F32),
            dma((3,)),
            dma((7, GROUP)),
            dma((7, GROUP)),
            dma((2, planes)),
            dma((2, planes)),
            dma((2, planes)),
            dma((2, planes)),
            dma,
            dma,
        ],
        compiler_params=pltpu.CompilerParams(
            collective_id=0, has_side_effects=True, vmem_limit_bytes=40 * 1024 * 1024
        ),
        cost_estimate=pl.CostEstimate(
            flops=8 * images * width * hidden_dev,
            bytes_accessed=40 * depth * hidden_dev,
            transcendentals=2 * images * hidden_dev,
        ),
    )(normed, residual_in, w_up, w_down.T, head_pair)


def plain_front(normed, residual_in, w_up, w_down, head_pair):
    images = normed.shape[0]
    logits = head_pair.shape[0] // 2
    up_pre = jnp.dot(
        normed, lax.all_gather(w_up, "dp", axis=0, tiled=True), preferred_element_type=F32
    )
    activ, slope = gelu_parts(up_pre)
    down_full = lax.all_gather(w_down, "dp", axis=1, tiled=True)
    partial_out = jnp.dot(activ.astype(BF16), down_full, preferred_element_type=F32)
    block_out = residual_in.astype(F32) + lax.psum(partial_out, "tensor")
    xhat, inv_std = normalize(block_out)
    both = jnp.concatenate([head_pair, xhat.astype(BF16)], axis=0)
    out = lax.dot_general(both, down_full, (((1,), (1,)), ((), ())), preferred_element_type=F32)
    head_back = out[:logits] + out[logits : 2 * logits]
    return jnp.concatenate([slope, head_back], axis=0), out[2 * logits :], xhat, inv_std


def from_first(value, ranks, tensor_rank):
    if ranks == 2:
        other = lax.ppermute(value, "tensor", [(0, 1)])
        return jnp.where(tensor_rank == 0, value, other)
    return lax.psum(jnp.where(tensor_rank == 0, value, jnp.zeros_like(value)), "tensor")


def body(
    members,
    ranks,
    normed,
    residual_in,
    w_up,
    w_down,
    final_gain,
    head_cols,
    sub_inputs,
    sub_hidden,
    panels,
    inverses,
):
    images, width = normed.shape
    hidden_dev = w_up.shape[1]
    logits = head_cols.shape[1]
    panel = inverses.shape[1]
    rows_dev = sub_inputs.shape[0]
    tensor_rank = lax.axis_index("tensor")

    corner = from_first(panels[0, :, panel : 2 * panel], ranks, tensor_rank)
    joined = jnp.concatenate([panels[0], panels[1], corner], axis=1)
    gathered = lax.all_gather(joined, "dp", axis=0, tiled=True)

    scaled_head = (final_gain[:, None] * head_cols.astype(F32)).T
    centred_head = scaled_head - jnp.mean(scaled_head, axis=1, keepdims=True)
    head_high = centred_head.astype(BF16)
    head_low = (centred_head - head_high.astype(F32)).astype(BF16)
    head_pair = jnp.concatenate([head_high, head_low], axis=0)

    fits = (
        ranks == 2
        and members % GROUP == 0
        and hidden_dev % (GROUP * 128) == 0
        and w_up.shape[0] % 16 == 0
        and images % 16 == 0
    )
    if fits:
        side, back, xhat, inv_std = fused_front(
            normed, residual_in, w_up, w_down, head_pair, members
        )
    else:
        side, back, xhat, inv_std = plain_front(normed, residual_in, w_up, w_down, head_pair)
    inv_std = inv_std[:, :1]
    project = (
        lax.dot_general(
            xhat, scaled_head, (((1,), (1,)), ((), ())), precision=lax.Precision.HIGHEST
        )
        / width
    )
    picked = jnp.take(normed, sub_inputs, axis=1).astype(F32)
    local_hidden = sub_hidden - tensor_rank * hidden_dev
    chosen = jnp.take(jnp.concatenate([side, back], axis=0), local_hidden, axis=1)
    gain = chosen[:images] * picked * inv_std
    head_back = chosen[images : images + logits]
    bent = chosen[images + logits :]

    def jacobian(gain, head_back, bent):
        return (
            gain[:, None, :] * (head_back[None, :, :] - project[:, :, None] * bent[:, None, :])
        ).astype(BF16).reshape(images * logits, gain.shape[1])

    packed = jnp.concatenate([gain, head_back, bent], axis=0)[:, : 2 * panel]
    packed = from_first(packed, ranks, tensor_rank)
    top = jacobian(packed[:images], packed[images : images + logits], packed[images + logits :])
    jac = jacobian(gain, head_back, bent)

    def solve(block, inverse):
        return lax.dot_general(
            block, inverse, (((1,), (1,)), ((), ())), preferred_element_type=F32
        ).astype(BF16)

    first = solve(top[:, :panel], inverses[0])
    second_in = top[:, panel:].astype(F32) - jnp.dot(
        first, gathered[:, 2 * rows_dev :], preferred_element_type=F32
    )
    second = solve(second_in.astype(BF16), inverses[1])
    solved = jnp.concatenate([first, second], axis=1)
    lower = jnp.concatenate([gathered[:, :rows_dev], gathered[:, rows_dev : 2 * rows_dev]], axis=0)
    update = jnp.dot(solved, lower, preferred_element_type=F32)
    below = (jac.astype(F32) - update).astype(BF16)
    head_part = jnp.where(tensor_rank == 0, solved, below[:, : 2 * panel])
    result = jnp.concatenate([head_part, below[:, 2 * panel :]], axis=1)
    return result.reshape(images, logits, rows_dev)


def solution(mesh):
    in_specs = (
        P("dp", None),
        P("dp", None),
        P("dp", "tensor"),
        P("tensor", "dp"),
        P(),
        P(),
        P("tensor"),
        P("tensor"),
        P(None, "dp", "tensor"),
        P(),
    )
    out_specs = P("dp", None, "tensor")
    return jax.shard_map(
        functools.partial(body, mesh.shape["dp"], mesh.shape["tensor"]),
        mesh=mesh, in_specs=in_specs, out_specs=out_specs, check_vma=False,
    )
```

```python
import functools

import jax
import jax.numpy as jnp
from jax import lax
from jax.experimental import pallas as pl
from jax.experimental.pallas import tpu as pltpu
from jax.sharding import PartitionSpec as P

MESH = pl.DeviceIdType.MESH
GROUP = 4
F32 = jnp.float32
BF16 = jnp.bfloat16


def gelu_parts(values):
    normal_cdf = 0.5 * (1.0 + lax.erf(values * 0.7071067811865476))
    slope = normal_cdf + values * jnp.exp(-0.5 * values * values) * 0.3989422804014327
    return (values * normal_cdf, slope)


def normalize(block_result):
    mean_x = jnp.mean(block_result, axis=1, keepdims=True)
    centred = block_result - mean_x
    inv_std = lax.rsqrt(jnp.mean(centred * centred, axis=1, keepdims=True) + 1e-06)
    return centred * inv_std, inv_std


def halves(values):
    high = values.astype(BF16)
    return high, (values - high.astype(F32)).astype(BF16)


def pick_columns(values, index, size):
    where = lax.broadcasted_iota(jnp.int32, (size, index.shape[1]), 0)
    chosen = jnp.where(where == index, 1.0, 0.0).astype(BF16)
    return jnp.dot(values, chosen, preferred_element_type=F32)


def front_kernel(
    planes,
    panel,
    normed_hbm, resid_hbm, wup_ref, wdt_ref, gain_ref, head_ref, inputs_ref, units_ref,
    pick_ref, top_ref, project_ref,
    normed_ref, resid_ref, nall, wu, wd, part, parts_in, pair_out, pair_in, xown, xall,
    side_src, side_in, back_src, back_in, onehot, xsum, pick_out, pick_in,
    local_sem, flat_send, flat_recv, up_send, up_recv, dn_send, dn_recv, pair_send, pair_recv,
):
    d = lax.axis_index("dp")
    t = lax.axis_index("tensor")
    z = d // GROUP
    p = lax.rem(d, GROUP)
    images, width = normed_ref.shape
    cols = wu.shape[3]
    logits = head_ref.shape[0]
    last = planes - 1
    others = range(1, GROUP)

    barrier = pltpu.get_barrier_semaphore()
    for o in others:
        pl.semaphore_signal(barrier, inc=1, device_id=(z * GROUP + (p ^ o), t), device_id_type=MESH)
    pl.semaphore_signal(barrier, inc=1, device_id=(d, 1 - t), device_id_type=MESH)

    @pl.when(z > 0)
    def _():
        pl.semaphore_signal(barrier, inc=1, device_id=(d - GROUP, t), device_id_type=MESH)

    @pl.when(z < last)
    def _():
        pl.semaphore_signal(barrier, inc=1, device_id=(d + GROUP, t), device_id_type=MESH)

    pl.semaphore_wait(barrier, GROUP + jnp.where(z > 0, 1, 0) + jnp.where(z < last, 1, 0))

    def flat(src, dst, kind, o):
        return pltpu.make_async_remote_copy(
            src_ref=src, dst_ref=dst, send_sem=flat_send.at[kind, o], recv_sem=flat_recv.at[kind, o],
            device_id=(z * GROUP + (p ^ o), t), device_id_type=MESH,
        )

    def block(ref, q):
        return ref.at[:, pl.ds(pl.multiple_of(q * cols, 128), cols)]

    sent = []
    own = [
        pltpu.make_async_copy(block(wup_ref, p), wu.at[z, p], local_sem.at[0]),
        pltpu.make_async_copy(block(wdt_ref, p), wd.at[z, p], local_sem.at[1]),
        pltpu.make_async_copy(normed_hbm, normed_ref, local_sem.at[2]),
        pltpu.make_async_copy(resid_hbm, resid_ref, local_sem.at[3]),
    ]
    moves = {}

    def spread(kind, pick, dst):
        for o in others:
            copy = flat(pick(p ^ o), dst, kind, o)
            copy.start()
            moves[kind, o] = copy
            sent.append(copy)

    def landed(kind):
        for o in others:
            moves[kind, o].wait_recv()

    spread(0, lambda q: block(wup_ref, q), wu.at[z, p])
    for copy in own:
        copy.start()
    own[2].wait()
    own[3].wait()
    nall[p] = normed_ref[...]
    head = head_ref[...].astype(F32) * gain_ref[...]
    head = head - jnp.mean(head, axis=1, keepdims=True)
    head_high, head_low = halves(head)
    head_pair = jnp.concatenate([head_high, head_low], axis=0)

    def hop(buf, w, src, s, step):
        send, recv = (up_send, up_recv) if step > 0 else (dn_send, dn_recv)
        return pltpu.make_async_remote_copy(
            src_ref=buf.at[src], dst_ref=buf.at[src], send_sem=send.at[w, s], recv_sem=recv.at[w, s],
            device_id=(d + step * GROUP, t), device_id_type=MESH,
        )

    def relay(buf, w, s):
        @pl.when(z >= s)
        def _():
            if s > 0:
                hop(buf, w, z - s, s - 1, 1).wait_recv()

            @pl.when(z < last)
            def _():
                hop(buf, w, z - s, s, 1).start()

        @pl.when(z + s <= last)
        def _():
            if s > 0:
                hop(buf, w, z + s, s - 1, -1).wait_recv()

            @pl.when(z > 0)
            def _():
                hop(buf, w, z + s, s, -1).start()

    own[0].wait()
    landed(0)
    relay(wu, 0, 0)
    spread(1, lambda q: block(wdt_ref, q), wd.at[z, p])
    own[1].wait()
    landed(1)
    relay(wd, 1, 0)
    spread(2, lambda q: normed_ref, nall.at[p])
    picked = pick_columns(normed_ref[...], inputs_ref[...], width)
    chunk = lax.broadcasted_iota(jnp.int32, (cols, units_ref.shape[1]), 0)
    relay(wu, 0, 1)
    for q in range(GROUP):
        onehot[q] = jnp.where(chunk + q * cols == units_ref[...], 1.0, 0.0).astype(BF16)
    landed(2)
    for s in range(2, planes):
        relay(wu, 0, s)

    rows = GROUP * images
    up_pre = jnp.dot(
        nall[...].reshape(rows, width), wu[...].reshape(width, cols), preferred_element_type=F32
    )
    activ, slope = gelu_parts(up_pre)
    hidden = activ.astype(BF16)
    side_src[:, :images, :] = slope.reshape(GROUP, images, cols)

    for s in range(1, planes):
        relay(wd, 1, s)
    down = wd[...].reshape(width, cols)
    partial = lax.dot_general(hidden, down, (((1,), (1,)), ((), ())), preferred_element_type=F32)
    pair_out[...] = partial.reshape(GROUP, images, width)
    part[...] = partial.astype(BF16).reshape(GROUP, images, width)
    for o in others:
        copy = flat(part.at[p ^ o], parts_in.at[o - 1], 3, o)
        copy.start()
        moves[3, o] = copy
        sent.append(copy)
    head_back = jnp.dot(head_pair, down, preferred_element_type=F32)
    head_back = head_back[:logits] + head_back[logits:]
    for q in range(GROUP):
        side_src[q, images:, :] = head_back
    total = pair_out[p]
    for o in others:
        moves[3, o].wait_recv()
        total = total + parts_in[o - 1].astype(F32)
    xsum[...] = total
    swap = pltpu.make_async_remote_copy(
        src_ref=xsum, dst_ref=pair_in, send_sem=pair_send.at[0], recv_sem=pair_recv.at[0],
        device_id=(d, 1 - t), device_id_type=MESH,
    )
    swap.start()
    swap.wait()
    block_out = resid_ref[...].astype(F32) + (xsum[...] + pair_in[...])
    xhat, inv_std = normalize(block_out)
    xown[...] = xhat.astype(BF16)
    spread(4, lambda q: xown, xall.at[p])
    spread(5, lambda q: side_src.at[q], side_in.at[p])
    xall[p] = xown[...]
    side_in[p] = side_src[p]
    x_high, x_low = halves(xhat)
    nums = (((1,), (1,)), ((), ()))
    project = lax.dot_general(x_high, head_high, nums, preferred_element_type=F32)
    project += lax.dot_general(x_low, head_high, nums, preferred_element_type=F32)
    project += lax.dot_general(x_high, head_low, nums, preferred_element_type=F32)
    project_ref[...] = project * (1.0 / width)
    landed(4)
    back = jnp.dot(xall[...].reshape(rows, width), down, preferred_element_type=F32)
    back_src[...] = back.reshape(GROUP, images, cols)
    spread(6, lambda q: back_src.at[q], back_in.at[p])
    back_in[p] = back_src[p]
    landed(5)
    chosen = jnp.zeros((2 * (images + logits), units_ref.shape[1]), F32)
    for q in range(GROUP):
        both = jnp.concatenate(halves(side_in[q]), axis=0)
        chosen += jnp.dot(both, onehot[q], preferred_element_type=F32)
    chosen = chosen[: images + logits] + chosen[images + logits :]
    pick_ref[:images] = chosen[:images] * picked * inv_std
    pick_ref[images : images + logits] = chosen[images:]
    landed(6)
    chosen = jnp.zeros((2 * images, units_ref.shape[1]), F32)
    for q in range(GROUP):
        both = jnp.concatenate(halves(back_in[q]), axis=0)
        chosen += jnp.dot(both, onehot[q], preferred_element_type=F32)
    pick_ref[images + logits :] = chosen[:images] + chosen[images:]
    pick_out[...] = pick_ref[:, : 2 * panel]
    swap = pltpu.make_async_remote_copy(
        src_ref=pick_out, dst_ref=pick_in, send_sem=pair_send.at[1], recv_sem=pair_recv.at[1],
        device_id=(d, 1 - t), device_id_type=MESH,
    )
    swap.start()
    swap.wait()
    top_ref[...] = jnp.where(t == 0, pick_out[...], pick_in[...])
    for copy in sent:
        copy.wait_send()
    for w, buf in enumerate((wu, wd)):
        for s in range(planes):
            @pl.when((z >= s) & (z < last))
            def _():
                hop(buf, w, z - s, s, 1).wait_send()

            @pl.when((z + s <= last) & (z > 0))
            def _():
                hop(buf, w, z + s, s, -1).wait_send()


def fused_front(normed, residual_in, w_up, w_down, gain, head, inputs, units, members, panel):
    images, width = normed.shape
    depth, hidden_dev = w_up.shape
    logits = head.shape[0]
    rows_dev = units.shape[1]
    planes = members // GROUP
    cols = hidden_dev // GROUP
    side = images + logits
    total = side + images
    dma = pltpu.SemaphoreType.DMA
    vmem = pl.BlockSpec(memory_space=pltpu.VMEM)
    hbm = pl.BlockSpec(memory_space=pltpu.HBM)
    return pl.pallas_call(
        functools.partial(front_kernel, planes, panel),
        out_shape=(
            jax.ShapeDtypeStruct((total, rows_dev), F32),
            jax.ShapeDtypeStruct((total, 2 * panel), F32),
            jax.ShapeDtypeStruct((images, logits), F32),
        ),
        in_specs=[hbm] * 4 + [vmem] * 4,
        out_specs=(vmem,) * 3,
        scratch_shapes=[
            pltpu.VMEM((images, width), BF16),
            pltpu.VMEM((images, width), BF16),
            pltpu.VMEM((GROUP, images, width), BF16),
            pltpu.VMEM((planes, GROUP, depth, cols), BF16),
            pltpu.VMEM((planes, GROUP, depth, cols), BF16),
            pltpu.VMEM((GROUP, images, width), BF16),
            pltpu.VMEM((GROUP - 1, images, width), BF16),
            pltpu.VMEM((GROUP, images, width), F32),
            pltpu.VMEM((images, width), F32),
            pltpu.VMEM((images, width), BF16),
            pltpu.VMEM((GROUP, images, width), BF16),
            pltpu.VMEM((GROUP, side, cols), F32),
            pltpu.VMEM((GROUP, side, cols), F32),
            pltpu.VMEM((GROUP, images, cols), F32),
            pltpu.VMEM((GROUP, images, cols), F32),
            pltpu.VMEM((GROUP, cols, rows_dev), BF16),
            pltpu.VMEM((images, width), F32),
            pltpu.VMEM((total, 2 * panel), F32),
            pltpu.VMEM((total, 2 * panel), F32),
            dma((4,)),
            dma((7, GROUP)),
            dma((7, GROUP)),
            dma((2, planes)),
            dma((2, planes)),
            dma((2, planes)),
            dma((2, planes)),
            dma((2,)),
            dma((2,)),
        ],
        compiler_params=pltpu.CompilerParams(
            collective_id=0, has_side_effects=True, vmem_limit_bytes=48 * 1024 * 1024
        ),
        cost_estimate=pl.CostEstimate(
            flops=16 * images * width * hidden_dev,
            bytes_accessed=800 * depth * hidden_dev,
            transcendentals=2 * images * hidden_dev,
        ),
    )(normed, residual_in, w_up, w_down.T, gain, head, inputs, units)


def tail_kernel(
    panel, gain_ref, bent_ref, head_ref, top_gain_ref, top_bent_ref, top_head_ref, project_ref,
    panels_ref, corner_ref, inverses_ref, out_ref,
):
    t = lax.axis_index("tensor")
    images, rows_dev = gain_ref.shape
    logits = head_ref.shape[0]
    project = project_ref[...].reshape(images, logits, 1)

    def jacobian(gain, head, bent):
        value = gain[:, None, :] * (head[None, :, :] - project * bent[:, None, :])
        return value.reshape(images * logits, gain.shape[1]).astype(BF16)

    def solve(block, inverse):
        return lax.dot_general(
            block, inverse, (((1,), (1,)), ((), ())), preferred_element_type=F32
        ).astype(BF16)

    top = jacobian(top_gain_ref[...], top_head_ref[...], top_bent_ref[...])
    first = solve(top[:, :panel], inverses_ref[0])
    second_in = top[:, panel:].astype(F32) - jnp.dot(
        first, corner_ref[...], preferred_element_type=F32
    )
    second = solve(second_in.astype(BF16), inverses_ref[1])
    solved = jnp.concatenate([first, second], axis=1)
    lower = panels_ref[...].reshape(2 * panel, rows_dev)
    update = jnp.dot(solved, lower, preferred_element_type=F32)
    jac = jacobian(gain_ref[...], head_ref[...], bent_ref[...])
    below = jac.astype(F32) - update
    out_ref[:, 2 * panel :] = below[:, 2 * panel :].astype(BF16)
    out_ref[:, : 2 * panel] = jnp.where(
        t == 0, solved.astype(F32), below[:, : 2 * panel]
    ).astype(BF16)


def tail(pick, top, project, gathered, corner, inverses, images, logits):
    panel = inverses.shape[1]
    rows_dev = pick.shape[1]
    step = 16 if images % 16 == 0 else images

    def rows(count, columns):
        return pl.BlockSpec((count, columns), lambda i: (i, 0))

    def whole(*shape):
        return pl.BlockSpec(shape, lambda i: (0,) * len(shape))

    def cut(values):
        return values[:images], values[images + logits :], values[images : images + logits]

    return pl.pallas_call(
        functools.partial(tail_kernel, panel),
        grid=(images // step,),
        out_shape=jax.ShapeDtypeStruct((images * logits, rows_dev), BF16),
        in_specs=[
            rows(step, rows_dev), rows(step, rows_dev), whole(logits, rows_dev),
            rows(step, 2 * panel), rows(step, 2 * panel), whole(logits, 2 * panel),
            rows(step * logits, 1),
            whole(2, panel, rows_dev), whole(panel, panel), whole(2, panel, panel),
        ],
        out_specs=rows(step * logits, rows_dev),
        compiler_params=pltpu.CompilerParams(vmem_limit_bytes=40 * 1024 * 1024),
    )(
        *cut(pick), *cut(top), project.reshape(images * logits, 1), gathered, corner, inverses
    )


def plain_front(normed, residual_in, w_up, w_down, head_pair):
    images = normed.shape[0]
    logits = head_pair.shape[0] // 2
    up_pre = jnp.dot(
        normed, lax.all_gather(w_up, "dp", axis=0, tiled=True), preferred_element_type=F32
    )
    activ, slope = gelu_parts(up_pre)
    down_full = lax.all_gather(w_down, "dp", axis=1, tiled=True)
    partial_out = jnp.dot(activ.astype(BF16), down_full, preferred_element_type=F32)
    block_out = residual_in.astype(F32) + lax.psum(partial_out, "tensor")
    xhat, inv_std = normalize(block_out)
    both = jnp.concatenate([head_pair, xhat.astype(BF16)], axis=0)
    out = lax.dot_general(both, down_full, (((1,), (1,)), ((), ())), preferred_element_type=F32)
    head_back = out[:logits] + out[logits : 2 * logits]
    return jnp.concatenate([slope, head_back], axis=0), out[2 * logits :], xhat, inv_std


def from_first(value, ranks, tensor_rank):
    if ranks == 2:
        other = lax.ppermute(value, "tensor", [(0, 1)])
        return jnp.where(tensor_rank == 0, value, other)
    return lax.psum(jnp.where(tensor_rank == 0, value, jnp.zeros_like(value)), "tensor")


def body(
    members,
    ranks,
    normed,
    residual_in,
    w_up,
    w_down,
    final_gain,
    head_cols,
    sub_inputs,
    sub_hidden,
    panels,
    inverses,
):
    images, width = normed.shape
    hidden_dev = w_up.shape[1]
    logits = head_cols.shape[1]
    panel = inverses.shape[1]
    rows_dev = sub_inputs.shape[0]
    tensor_rank = lax.axis_index("tensor")

    gathered = lax.all_gather(panels, "dp", axis=1, tiled=True)
    corner = from_first(gathered[0, :, panel : 2 * panel], ranks, tensor_rank)
    local_hidden = sub_hidden - tensor_rank * hidden_dev

    fits = (
        ranks == 2
        and members % GROUP == 0
        and hidden_dev % (GROUP * 128) == 0
        and w_up.shape[0] % 16 == 0
        and images % 16 == 0
    )
    if fits:
        pick, top, project = fused_front(
            normed, residual_in, w_up, w_down, final_gain[None, :], head_cols.T,
            sub_inputs[None, :], local_hidden[None, :], members, panel,
        )
    else:
        scaled_head = (final_gain[:, None] * head_cols.astype(F32)).T
        centred_head = scaled_head - jnp.mean(scaled_head, axis=1, keepdims=True)
        head_pair = jnp.concatenate(halves(centred_head), axis=0)
        side, back, xhat, inv_std = plain_front(normed, residual_in, w_up, w_down, head_pair)
        project = lax.dot_general(
            xhat, centred_head, (((1,), (1,)), ((), ())), precision=lax.Precision.HIGHEST
        ) / width
        picked = jnp.take(normed, sub_inputs, axis=1).astype(F32)
        chosen = jnp.take(jnp.concatenate([side, back], axis=0), local_hidden, axis=1)
        pick = jnp.concatenate([chosen[:images] * picked * inv_std, chosen[images:]], axis=0)
        top = from_first(pick[:, : 2 * panel], ranks, tensor_rank)
    result = tail(pick, top, project, gathered, corner, inverses, images, logits)
    return result.reshape(images, logits, rows_dev)


def solution(mesh):
    in_specs = (
        P("dp", None),
        P("dp", None),
        P("dp", "tensor"),
        P("tensor", "dp"),
        P(),
        P(),
        P("tensor"),
        P("tensor"),
        P(None, "dp", "tensor"),
        P(),
    )
    out_specs = P("dp", None, "tensor")
    return jax.shard_map(
        functools.partial(body, mesh.shape["dp"], mesh.shape["tensor"]),
        mesh=mesh, in_specs=in_specs, out_specs=out_specs, check_vma=False,
    )
```

```python
import functools

import jax
import jax.numpy as jnp
from jax import lax
from jax.experimental import pallas as pl
from jax.experimental.pallas import tpu as pltpu
from jax.sharding import PartitionSpec as P

MESH = pl.DeviceIdType.MESH
GROUP = 4
F32 = jnp.float32
BF16 = jnp.bfloat16


def gelu_parts(values):
    normal_cdf = 0.5 * (1.0 + lax.erf(values * 0.7071067811865476))
    slope = normal_cdf + values * jnp.exp(-0.5 * values * values) * 0.3989422804014327
    return (values * normal_cdf, slope)


def normalize(block_result):
    mean_x = jnp.mean(block_result, axis=1, keepdims=True)
    centred = block_result - mean_x
    inv_std = lax.rsqrt(jnp.mean(centred * centred, axis=1, keepdims=True) + 1e-06)
    return centred * inv_std, inv_std


def halves(values):
    high = values.astype(BF16)
    return high, (values - high.astype(F32)).astype(BF16)


def pick_columns(values, index, size):
    where = lax.broadcasted_iota(jnp.int32, (size, index.shape[1]), 0)
    chosen = jnp.where(where == index, 1.0, 0.0).astype(BF16)
    return jnp.dot(values, chosen, preferred_element_type=F32)


def front_kernel(
    planes,
    panel,
    normed_hbm, resid_hbm, wup_ref, wdt_ref, gain_ref, head_ref, inputs_ref, units_ref, panels_hbm,
    pick_ref, top_ref, project_ref, panels_ref, corner_ref,
    normed_ref, resid_ref, nall, wu, wd, part, parts_in, pair_out, pair_in, xown, xall,
    slope_src, slope_in, head_src, head_in, back_src, back_in, onehot, xsum, pick_out, pick_in,
    pan, corner_out, corner_in,
    local_sem, flat_send, flat_recv, up_send, up_recv, dn_send, dn_recv, pair_send, pair_recv,
):
    d = lax.axis_index("dp")
    t = lax.axis_index("tensor")
    z = d // GROUP
    p = lax.rem(d, GROUP)
    images, width = normed_ref.shape
    cols = wu.shape[3]
    logits = head_ref.shape[0]
    last = planes - 1
    others = range(1, GROUP)

    barrier = pltpu.get_barrier_semaphore()
    for o in others:
        pl.semaphore_signal(barrier, inc=1, device_id=(z * GROUP + (p ^ o), t), device_id_type=MESH)
    pl.semaphore_signal(barrier, inc=1, device_id=(d, 1 - t), device_id_type=MESH)

    @pl.when(z > 0)
    def _():
        pl.semaphore_signal(barrier, inc=1, device_id=(d - GROUP, t), device_id_type=MESH)

    @pl.when(z < last)
    def _():
        pl.semaphore_signal(barrier, inc=1, device_id=(d + GROUP, t), device_id_type=MESH)

    pl.semaphore_wait(barrier, GROUP + jnp.where(z > 0, 1, 0) + jnp.where(z < last, 1, 0))

    def flat(src, dst, kind, o):
        return pltpu.make_async_remote_copy(
            src_ref=src, dst_ref=dst, send_sem=flat_send.at[kind, o], recv_sem=flat_recv.at[kind, o],
            device_id=(z * GROUP + (p ^ o), t), device_id_type=MESH,
        )

    def block(ref, q):
        return ref.at[:, pl.ds(pl.multiple_of(q * cols, 128), cols)]

    sent = []
    own = [
        pltpu.make_async_copy(block(wup_ref, p), wu.at[z, p], local_sem.at[0]),
        pltpu.make_async_copy(block(wdt_ref, p), wd.at[z, p], local_sem.at[1]),
        pltpu.make_async_copy(normed_hbm, normed_ref, local_sem.at[2]),
        pltpu.make_async_copy(resid_hbm, resid_ref, local_sem.at[3]),
        pltpu.make_async_copy(panels_hbm, pan.at[z, p], local_sem.at[4]),
    ]
    moves = {}

    def spread(kind, pick, dst):
        for o in others:
            copy = flat(pick(p ^ o), dst, kind, o)
            copy.start()
            moves[kind, o] = copy
            sent.append(copy)

    def landed(kind):
        for o in others:
            moves[kind, o].wait_recv()

    spread(0, lambda q: block(wup_ref, q), wu.at[z, p])
    for copy in own:
        copy.start()
    own[2].wait()
    own[3].wait()
    nall[p] = normed_ref[...]
    head = head_ref[...].astype(F32) * gain_ref[...]
    head = head - jnp.mean(head, axis=1, keepdims=True)
    head_high, head_low = halves(head)
    head_pair = jnp.concatenate([head_high, head_low], axis=0)

    def selected(parts):
        chosen = 0.0
        for q in range(GROUP):
            both = jnp.concatenate(halves(parts[q]), axis=0)
            chosen += jnp.dot(both, onehot[q], preferred_element_type=F32)
        count = parts.shape[1]
        return chosen[:count] + chosen[count:]

    def hop(buf, w, src, s, step):
        send, recv = (up_send, up_recv) if step > 0 else (dn_send, dn_recv)
        return pltpu.make_async_remote_copy(
            src_ref=buf.at[src], dst_ref=buf.at[src], send_sem=send.at[w, s], recv_sem=recv.at[w, s],
            device_id=(d + step * GROUP, t), device_id_type=MESH,
        )

    def relay(buf, w, s):
        @pl.when(z >= s)
        def _():
            if s > 0:
                hop(buf, w, z - s, s - 1, 1).wait_recv()

            @pl.when(z < last)
            def _():
                hop(buf, w, z - s, s, 1).start()

        @pl.when(z + s <= last)
        def _():
            if s > 0:
                hop(buf, w, z + s, s - 1, -1).wait_recv()

            @pl.when(z > 0)
            def _():
                hop(buf, w, z + s, s, -1).start()

    own[0].wait()
    landed(0)
    relay(wu, 0, 0)
    spread(1, lambda q: block(wdt_ref, q), wd.at[z, p])
    own[1].wait()
    landed(1)
    relay(wd, 1, 0)
    spread(2, lambda q: normed_ref, nall.at[p])
    spread(7, lambda q: panels_hbm, pan.at[z, p])
    own[4].wait()
    picked = pick_columns(normed_ref[...], inputs_ref[...], width)
    chunk = lax.broadcasted_iota(jnp.int32, (cols, units_ref.shape[1]), 0)
    relay(wu, 0, 1)
    for q in range(GROUP):
        onehot[q] = jnp.where(chunk + q * cols == units_ref[...], 1.0, 0.0).astype(BF16)
    landed(2)
    for s in range(2, planes):
        relay(wu, 0, s)
        if s == 2:
            relay(wd, 1, 1)

    rows = GROUP * images
    up_pre = jnp.dot(
        nall[...].reshape(rows, width), wu[...].reshape(width, cols), preferred_element_type=F32
    )
    activ, slope = gelu_parts(up_pre)
    hidden = activ.astype(BF16)
    slope_src[...] = slope.reshape(GROUP, images, cols)
    spread(5, lambda q: slope_src.at[q], slope_in.at[p])
    slope_in[p] = slope_src[p]
    for s in range(2, planes - 1):
        relay(wd, 1, s)
    landed(5)
    pick_ref[:images] = selected(slope_in) * picked
    landed(7)
    relay(wd, 1, planes - 1)
    relay(pan, 2, 0)
    down = wd[...].reshape(width, cols)
    partial = lax.dot_general(hidden, down, (((1,), (1,)), ((), ())), preferred_element_type=F32)
    pair_out[...] = partial.reshape(GROUP, images, width)
    part[...] = partial.astype(BF16).reshape(GROUP, images, width)
    for o in others:
        copy = flat(part.at[p ^ o], parts_in.at[o - 1], 3, o)
        copy.start()
        moves[3, o] = copy
        sent.append(copy)
    head_back = jnp.dot(head_pair, down, preferred_element_type=F32)
    head_back = head_back[:logits] + head_back[logits:]
    head_src[...] = head_back
    spread(8, lambda q: head_src, head_in.at[p])
    head_in[p] = head_back
    total = pair_out[p]
    for o in others:
        moves[3, o].wait_recv()
        total = total + parts_in[o - 1].astype(F32)
    xsum[...] = total
    swap = pltpu.make_async_remote_copy(
        src_ref=xsum, dst_ref=pair_in, send_sem=pair_send.at[0], recv_sem=pair_recv.at[0],
        device_id=(d, 1 - t), device_id_type=MESH,
    )
    swap.start()
    swap.wait()
    block_out = resid_ref[...].astype(F32) + (xsum[...] + pair_in[...])
    xhat, inv_std = normalize(block_out)
    xown[...] = xhat.astype(BF16)
    spread(4, lambda q: xown, xall.at[p])
    relay(pan, 2, 1)
    xall[p] = xown[...]
    x_high, x_low = halves(xhat)
    nums = (((1,), (1,)), ((), ()))
    project = lax.dot_general(x_high, head_high, nums, preferred_element_type=F32)
    project += lax.dot_general(x_low, head_high, nums, preferred_element_type=F32)
    project += lax.dot_general(x_high, head_low, nums, preferred_element_type=F32)
    project_ref[...] = project * (1.0 / width)
    landed(4)
    back = jnp.dot(xall[...].reshape(rows, width), down, preferred_element_type=F32)
    back_src[...] = back.astype(BF16).reshape(GROUP, images, cols)
    spread(6, lambda q: back_src.at[q], back_in.at[p])
    back_in[p] = back_src[p]
    landed(8)
    pick_ref[:images] = pick_ref[:images] * inv_std
    pick_ref[images : images + logits] = selected(head_in)
    for s in range(2, planes):
        relay(pan, 2, s)
    for q in range(2):
        panels_ref[q] = pan[:, :, q].reshape(panels_ref.shape[1:])
    corner_out[...] = panels_ref[0, :, panel : 2 * panel]

    def swap(src, dst, i):
        return pltpu.make_async_remote_copy(
            src_ref=src, dst_ref=dst, send_sem=pair_send.at[i], recv_sem=pair_recv.at[i],
            device_id=(d, 1 - t), device_id_type=MESH,
        )

    corner_swap = swap(corner_out, corner_in, 2)
    corner_swap.start()
    landed(6)
    chosen = jnp.zeros((images, units_ref.shape[1]), F32)
    for q in range(GROUP):
        chosen += jnp.dot(back_in[q], onehot[q], preferred_element_type=F32)
    pick_ref[images + logits :] = chosen
    pick_out[...] = pick_ref[:, : 2 * panel]
    pick_swap = swap(pick_out, pick_in, 1)
    pick_swap.start()
    corner_swap.wait()
    pick_swap.wait()
    top_ref[...] = jnp.where(t == 0, pick_out[...], pick_in[...])
    corner_ref[...] = jnp.where(
        t == 0, corner_out[...].astype(F32), corner_in[...].astype(F32)
    ).astype(BF16)
    for copy in sent:
        copy.wait_send()
    for w, buf in enumerate((wu, wd, pan)):
        for s in range(planes):
            @pl.when((z >= s) & (z < last))
            def _():
                hop(buf, w, z - s, s, 1).wait_send()

            @pl.when((z + s <= last) & (z > 0))
            def _():
                hop(buf, w, z + s, s, -1).wait_send()


def fused_front(normed, residual_in, w_up, w_down, gain, head, inputs, units, panels, members):
    images, width = normed.shape
    depth, hidden_dev = w_up.shape
    logits = head.shape[0]
    panel = panels.shape[1] * members
    rows_dev = units.shape[1]
    planes = members // GROUP
    cols = hidden_dev // GROUP
    side = images + logits
    total = side + images
    dma = pltpu.SemaphoreType.DMA
    vmem = pl.BlockSpec(memory_space=pltpu.VMEM)
    hbm = pl.BlockSpec(memory_space=pltpu.HBM)
    return pl.pallas_call(
        functools.partial(front_kernel, planes, panel),
        out_shape=(
            jax.ShapeDtypeStruct((total, rows_dev), F32),
            jax.ShapeDtypeStruct((total, 2 * panel), F32),
            jax.ShapeDtypeStruct((images, logits), F32),
            jax.ShapeDtypeStruct((2, panel, rows_dev), BF16),
            jax.ShapeDtypeStruct((panel, panel), BF16),
        ),
        in_specs=[hbm] * 4 + [vmem] * 4 + [hbm],
        out_specs=(vmem,) * 5,
        scratch_shapes=[
            pltpu.VMEM((images, width), BF16),
            pltpu.VMEM((images, width), BF16),
            pltpu.VMEM((GROUP, images, width), BF16),
            pltpu.VMEM((planes, GROUP, depth, cols), BF16),
            pltpu.VMEM((planes, GROUP, depth, cols), BF16),
            pltpu.VMEM((GROUP, images, width), BF16),
            pltpu.VMEM((GROUP - 1, images, width), BF16),
            pltpu.VMEM((GROUP, images, width), F32),
            pltpu.VMEM((images, width), F32),
            pltpu.VMEM((images, width), BF16),
            pltpu.VMEM((GROUP, images, width), BF16),
            pltpu.VMEM((GROUP, images, cols), F32),
            pltpu.VMEM((GROUP, images, cols), F32),
            pltpu.VMEM((logits, cols), F32),
            pltpu.VMEM((GROUP, logits, cols), F32),
            pltpu.VMEM((GROUP, images, cols), BF16),
            pltpu.VMEM((GROUP, images, cols), BF16),
            pltpu.VMEM((GROUP, cols, rows_dev), BF16),
            pltpu.VMEM((images, width), F32),
            pltpu.VMEM((total, 2 * panel), F32),
            pltpu.VMEM((total, 2 * panel), F32),
            pltpu.VMEM((planes, GROUP) + panels.shape, BF16),
            pltpu.VMEM((panel, panel), BF16),
            pltpu.VMEM((panel, panel), BF16),
            dma((5,)),
            dma((9, GROUP)),
            dma((9, GROUP)),
            dma((3, planes)),
            dma((3, planes)),
            dma((3, planes)),
            dma((3, planes)),
            dma((3,)),
            dma((3,)),
        ],
        compiler_params=pltpu.CompilerParams(
            collective_id=0, has_side_effects=True, vmem_limit_bytes=48 * 1024 * 1024
        ),
        cost_estimate=pl.CostEstimate(
            flops=16 * images * width * hidden_dev,
            bytes_accessed=800 * depth * hidden_dev,
            transcendentals=2 * images * hidden_dev,
        ),
    )(normed, residual_in, w_up, w_down.T, gain, head, inputs, units, panels)


def tail_kernel(
    panel, gain_ref, bent_ref, head_ref, top_gain_ref, top_bent_ref, top_head_ref, project_ref,
    panels_ref, corner_ref, inverses_ref, out_ref,
):
    t = lax.axis_index("tensor")
    images, rows_dev = gain_ref.shape
    logits = head_ref.shape[0]
    project = project_ref[...].reshape(images, logits, 1)

    def jacobian(gain, head, bent):
        value = gain[:, None, :] * (head[None, :, :] - project * bent[:, None, :])
        return value.reshape(images * logits, gain.shape[1]).astype(BF16)

    def solve(block, inverse):
        return lax.dot_general(
            block, inverse, (((1,), (1,)), ((), ())), preferred_element_type=F32
        ).astype(BF16)

    top = jacobian(top_gain_ref[...], top_head_ref[...], top_bent_ref[...])
    first = solve(top[:, :panel], inverses_ref[0])
    second_in = top[:, panel:].astype(F32) - jnp.dot(
        first, corner_ref[...], preferred_element_type=F32
    )
    second = solve(second_in.astype(BF16), inverses_ref[1])
    solved = jnp.concatenate([first, second], axis=1)
    lower = panels_ref[...].reshape(2 * panel, rows_dev)
    update = jnp.dot(solved, lower, preferred_element_type=F32)
    jac = jacobian(gain_ref[...], head_ref[...], bent_ref[...])
    below = jac.astype(F32) - update
    out_ref[:, 2 * panel :] = below[:, 2 * panel :].astype(BF16)
    out_ref[:, : 2 * panel] = jnp.where(
        t == 0, solved.astype(F32), below[:, : 2 * panel]
    ).astype(BF16)


def tail(pick, top, project, gathered, corner, inverses, images, logits):
    panel = inverses.shape[1]
    rows_dev = pick.shape[1]
    step = 16 if images % 16 == 0 else images

    def rows(count, columns):
        return pl.BlockSpec((count, columns), lambda i: (i, 0))

    def whole(*shape):
        return pl.BlockSpec(shape, lambda i: (0,) * len(shape))

    def cut(values):
        return values[:images], values[images + logits :], values[images : images + logits]

    return pl.pallas_call(
        functools.partial(tail_kernel, panel),
        grid=(images // step,),
        out_shape=jax.ShapeDtypeStruct((images * logits, rows_dev), BF16),
        in_specs=[
            rows(step, rows_dev), rows(step, rows_dev), whole(logits, rows_dev),
            rows(step, 2 * panel), rows(step, 2 * panel), whole(logits, 2 * panel),
            rows(step * logits, 1),
            whole(2, panel, rows_dev), whole(panel, panel), whole(2, panel, panel),
        ],
        out_specs=rows(step * logits, rows_dev),
        compiler_params=pltpu.CompilerParams(vmem_limit_bytes=40 * 1024 * 1024),
    )(
        *cut(pick), *cut(top), project.reshape(images * logits, 1), gathered, corner, inverses
    )


def plain_front(normed, residual_in, w_up, w_down, head_pair):
    images = normed.shape[0]
    logits = head_pair.shape[0] // 2
    up_pre = jnp.dot(
        normed, lax.all_gather(w_up, "dp", axis=0, tiled=True), preferred_element_type=F32
    )
    activ, slope = gelu_parts(up_pre)
    down_full = lax.all_gather(w_down, "dp", axis=1, tiled=True)
    partial_out = jnp.dot(activ.astype(BF16), down_full, preferred_element_type=F32)
    block_out = residual_in.astype(F32) + lax.psum(partial_out, "tensor")
    xhat, inv_std = normalize(block_out)
    both = jnp.concatenate([head_pair, xhat.astype(BF16)], axis=0)
    out = lax.dot_general(both, down_full, (((1,), (1,)), ((), ())), preferred_element_type=F32)
    head_back = out[:logits] + out[logits : 2 * logits]
    return jnp.concatenate([slope, head_back], axis=0), out[2 * logits :], xhat, inv_std


def from_first(value, tensor_rank):
    return lax.psum(jnp.where(tensor_rank == 0, value, jnp.zeros_like(value)), "tensor")


def body(
    members,
    ranks,
    normed,
    residual_in,
    w_up,
    w_down,
    final_gain,
    head_cols,
    sub_inputs,
    sub_hidden,
    panels,
    inverses,
):
    images, width = normed.shape
    hidden_dev = w_up.shape[1]
    logits = head_cols.shape[1]
    panel = inverses.shape[1]
    rows_dev = sub_inputs.shape[0]
    tensor_rank = lax.axis_index("tensor")

    local_hidden = sub_hidden - tensor_rank * hidden_dev

    fits = (
        ranks == 2
        and members % GROUP == 0
        and hidden_dev % (GROUP * 128) == 0
        and w_up.shape[0] % 16 == 0
        and images % 16 == 0
        and panels.shape[1] % 16 == 0
        and members >= 3 * GROUP
    )
    if fits:
        pick, top, project, gathered, corner = fused_front(
            normed, residual_in, w_up, w_down, final_gain[None, :], head_cols.T,
            sub_inputs[None, :], local_hidden[None, :], panels, members,
        )
    else:
        gathered = lax.all_gather(panels, "dp", axis=1, tiled=True)
        corner = from_first(gathered[0, :, panel : 2 * panel], tensor_rank)
        scaled_head = (final_gain[:, None] * head_cols.astype(F32)).T
        centred_head = scaled_head - jnp.mean(scaled_head, axis=1, keepdims=True)
        head_pair = jnp.concatenate(halves(centred_head), axis=0)
        side, back, xhat, inv_std = plain_front(normed, residual_in, w_up, w_down, head_pair)
        project = lax.dot_general(
            xhat, centred_head, (((1,), (1,)), ((), ())), precision=lax.Precision.HIGHEST
        ) / width
        picked = jnp.take(normed, sub_inputs, axis=1).astype(F32)
        chosen = jnp.take(jnp.concatenate([side, back], axis=0), local_hidden, axis=1)
        pick = jnp.concatenate([chosen[:images] * picked * inv_std, chosen[images:]], axis=0)
        top = from_first(pick[:, : 2 * panel], tensor_rank)
    result = tail(pick, top, project, gathered, corner, inverses, images, logits)
    return result.reshape(images, logits, rows_dev)


def solution(mesh):
    in_specs = (
        P("dp", None),
        P("dp", None),
        P("dp", "tensor"),
        P("tensor", "dp"),
        P(),
        P(),
        P("tensor"),
        P("tensor"),
        P(None, "dp", "tensor"),
        P(),
    )
    out_specs = P("dp", None, "tensor")
    return jax.shard_map(
        functools.partial(body, mesh.shape["dp"], mesh.shape["tensor"]),
        mesh=mesh, in_specs=in_specs, out_specs=out_specs, check_vma=False,
    )
```

```python
import functools

import jax
import jax.numpy as jnp
from jax import lax
from jax.experimental import pallas as pl
from jax.experimental.pallas import tpu as pltpu
from jax.sharding import PartitionSpec as P

MESH = pl.DeviceIdType.MESH
GROUP = 4
F32 = jnp.float32
BF16 = jnp.bfloat16


def gelu_parts(values):
    normal_cdf = 0.5 * (1.0 + lax.erf(values * 0.7071067811865476))
    slope = normal_cdf + values * jnp.exp(-0.5 * values * values) * 0.3989422804014327
    return (values * normal_cdf, slope)


def normalize(block_result):
    mean_x = jnp.mean(block_result, axis=1, keepdims=True)
    centred = block_result - mean_x
    inv_std = lax.rsqrt(jnp.mean(centred * centred, axis=1, keepdims=True) + 1e-06)
    return centred * inv_std, inv_std


def halves(values):
    high = values.astype(BF16)
    return high, (values - high.astype(F32)).astype(BF16)


def pick_columns(values, index, size):
    where = lax.broadcasted_iota(jnp.int32, (size, index.shape[1]), 0)
    chosen = jnp.where(where == index, 1.0, 0.0).astype(BF16)
    return jnp.dot(values, chosen, preferred_element_type=F32)


def front_kernel(
    planes,
    panel,
    normed_hbm, resid_hbm, wup_ref, wdt_ref, gain_ref, head_ref, inputs_ref, units_ref, panels_hbm,
    pick_ref, top_ref, project_ref, panels_ref, corner_ref,
    normed_ref, resid_ref, nall, wu, wd, part, parts_in, pair_out, pair_in, xown, xall,
    slope_src, slope_in, head_src, head_in, back_src, back_in, onehot, xsum, pick_out, pick_in,
    pan, corner_out, corner_in,
    local_sem, flat_send, flat_recv, up_send, up_recv, dn_send, dn_recv, pair_send, pair_recv,
):
    d = lax.axis_index("dp")
    t = lax.axis_index("tensor")
    z = d // GROUP
    p = lax.rem(d, GROUP)
    images, width = normed_ref.shape
    cols = wu.shape[3]
    logits = head_ref.shape[0]
    last = planes - 1
    others = range(1, GROUP)

    barrier = pltpu.get_barrier_semaphore()
    for o in others:
        pl.semaphore_signal(barrier, inc=1, device_id=(z * GROUP + (p ^ o), t), device_id_type=MESH)
    pl.semaphore_signal(barrier, inc=1, device_id=(d, 1 - t), device_id_type=MESH)

    @pl.when(z > 0)
    def _():
        pl.semaphore_signal(barrier, inc=1, device_id=(d - GROUP, t), device_id_type=MESH)

    @pl.when(z < last)
    def _():
        pl.semaphore_signal(barrier, inc=1, device_id=(d + GROUP, t), device_id_type=MESH)

    pl.semaphore_wait(barrier, GROUP + jnp.where(z > 0, 1, 0) + jnp.where(z < last, 1, 0))

    def flat(src, dst, kind, o):
        return pltpu.make_async_remote_copy(
            src_ref=src, dst_ref=dst, send_sem=flat_send.at[kind, o], recv_sem=flat_recv.at[kind, o],
            device_id=(z * GROUP + (p ^ o), t), device_id_type=MESH,
        )

    def block(ref, q):
        return ref.at[:, pl.ds(pl.multiple_of(q * cols, 128), cols)]

    sent = []
    own = [
        pltpu.make_async_copy(block(wup_ref, p), wu.at[z, p], local_sem.at[0]),
        pltpu.make_async_copy(block(wdt_ref, p), wd.at[z, p], local_sem.at[1]),
        pltpu.make_async_copy(normed_hbm, normed_ref, local_sem.at[2]),
        pltpu.make_async_copy(resid_hbm, resid_ref, local_sem.at[3]),
        pltpu.make_async_copy(panels_hbm, pan.at[z, p], local_sem.at[4]),
    ]
    moves = {}

    def spread(kind, pick, dst):
        for o in others:
            copy = flat(pick(p ^ o), dst, kind, o)
            copy.start()
            moves[kind, o] = copy
            sent.append(copy)

    def landed(kind):
        for o in others:
            moves[kind, o].wait_recv()

    spread(0, lambda q: block(wup_ref, q), wu.at[z, p])
    for copy in own:
        copy.start()
    def selected(parts):
        chosen = 0.0
        for q in range(GROUP):
            both = jnp.concatenate(halves(parts[q]), axis=0)
            chosen += jnp.dot(both, onehot[q], preferred_element_type=F32)
        count = parts.shape[1]
        return chosen[:count] + chosen[count:]

    def hop(buf, w, src, s, step):
        send, recv = (up_send, up_recv) if step > 0 else (dn_send, dn_recv)
        return pltpu.make_async_remote_copy(
            src_ref=buf.at[src], dst_ref=buf.at[src], send_sem=send.at[w, s], recv_sem=recv.at[w, s],
            device_id=(d + step * GROUP, t), device_id_type=MESH,
        )

    def chunk_out(buf, w, q):
        def send(step, sems, marks):
            pltpu.make_async_remote_copy(
                src_ref=buf.at[z, q], dst_ref=buf.at[z, q], send_sem=sems.at[w, 0],
                recv_sem=marks.at[w, 0], device_id=(d + step * GROUP, t), device_id_type=MESH,
            ).start()

        @pl.when(z < last)
        def _():
            send(1, up_send, up_recv)

        @pl.when(z > 0)
        def _():
            send(-1, dn_send, dn_recv)

    def relay(buf, w, s):
        @pl.when(z >= s)
        def _():
            if s > 0:
                hop(buf, w, z - s, s - 1, 1).wait_recv()

            @pl.when(z < last)
            def _():
                hop(buf, w, z - s, s, 1).start()

        @pl.when(z + s <= last)
        def _():
            if s > 0:
                hop(buf, w, z + s, s - 1, -1).wait_recv()

            @pl.when(z > 0)
            def _():
                hop(buf, w, z + s, s, -1).start()

    own[0].wait()
    chunk_out(wu, 0, p)
    for o in others:
        moves[0, o].wait_recv()
        chunk_out(wu, 0, p ^ o)
    spread(1, lambda q: block(wdt_ref, q), wd.at[z, p])
    own[1].wait()
    chunk_out(wd, 1, p)
    for o in others:
        moves[1, o].wait_recv()
        chunk_out(wd, 1, p ^ o)
    own[2].wait()
    own[3].wait()
    nall[p] = normed_ref[...]
    head = head_ref[...].astype(F32) * gain_ref[...]
    head = head - jnp.mean(head, axis=1, keepdims=True)
    head_high, head_low = halves(head)
    head_pair = jnp.concatenate([head_high, head_low], axis=0)
    spread(2, lambda q: normed_ref, nall.at[p])
    spread(7, lambda q: panels_hbm, pan.at[z, p])
    own[4].wait()
    picked = pick_columns(normed_ref[...], inputs_ref[...], width)
    chunk = lax.broadcasted_iota(jnp.int32, (cols, units_ref.shape[1]), 0)
    relay(wu, 0, 1)
    for q in range(GROUP):
        onehot[q] = jnp.where(chunk + q * cols == units_ref[...], 1.0, 0.0).astype(BF16)
    landed(2)
    for s in range(2, planes):
        relay(wu, 0, s)
        if s == 2:
            relay(wd, 1, 1)

    rows = GROUP * images
    up_pre = jnp.dot(
        nall[...].reshape(rows, width), wu[...].reshape(width, cols), preferred_element_type=F32
    )
    activ, slope = gelu_parts(up_pre)
    hidden = activ.astype(BF16)
    slope_src[...] = slope.reshape(GROUP, images, cols)
    spread(5, lambda q: slope_src.at[q], slope_in.at[p])
    slope_in[p] = slope_src[p]
    for s in range(2, planes - 1):
        relay(wd, 1, s)
    landed(5)
    pick_ref[:images] = selected(slope_in) * picked
    landed(7)
    relay(wd, 1, planes - 1)
    relay(pan, 2, 0)
    down = wd[...].reshape(width, cols)
    partial = lax.dot_general(hidden, down, (((1,), (1,)), ((), ())), preferred_element_type=F32)
    pair_out[...] = partial.reshape(GROUP, images, width)
    part[...] = partial.astype(BF16).reshape(GROUP, images, width)
    for o in others:
        copy = flat(part.at[p ^ o], parts_in.at[o - 1], 3, o)
        copy.start()
        moves[3, o] = copy
        sent.append(copy)
    head_back = jnp.dot(head_pair, down, preferred_element_type=F32)
    head_back = head_back[:logits] + head_back[logits:]
    head_src[...] = head_back
    spread(8, lambda q: head_src, head_in.at[p])
    head_in[p] = head_back
    total = pair_out[p]
    for o in others:
        moves[3, o].wait_recv()
        total = total + parts_in[o - 1].astype(F32)
    xsum[...] = total
    swap = pltpu.make_async_remote_copy(
        src_ref=xsum, dst_ref=pair_in, send_sem=pair_send.at[0], recv_sem=pair_recv.at[0],
        device_id=(d, 1 - t), device_id_type=MESH,
    )
    swap.start()
    swap.wait()
    block_out = resid_ref[...].astype(F32) + (xsum[...] + pair_in[...])
    xhat, inv_std = normalize(block_out)
    xown[...] = xhat.astype(BF16)
    spread(4, lambda q: xown, xall.at[p])
    relay(pan, 2, 1)
    xall[p] = xown[...]
    x_high, x_low = halves(xhat)
    nums = (((1,), (1,)), ((), ()))
    project = lax.dot_general(x_high, head_high, nums, preferred_element_type=F32)
    project += lax.dot_general(x_low, head_high, nums, preferred_element_type=F32)
    project += lax.dot_general(x_high, head_low, nums, preferred_element_type=F32)
    project_ref[...] = project * (1.0 / width)
    landed(4)
    back = jnp.dot(xall[...].reshape(rows, width), down, preferred_element_type=F32)
    back_src[...] = back.astype(BF16).reshape(GROUP, images, cols)
    spread(6, lambda q: back_src.at[q], back_in.at[p])
    back_in[p] = back_src[p]
    landed(8)
    pick_ref[:images] = pick_ref[:images] * inv_std
    pick_ref[images : images + logits] = selected(head_in)
    for s in range(2, planes):
        relay(pan, 2, s)
    for q in range(2):
        panels_ref[q] = pan[:, :, q].reshape(panels_ref.shape[1:])
    corner_out[...] = panels_ref[0, :, panel : 2 * panel]

    def swap(src, dst, i):
        return pltpu.make_async_remote_copy(
            src_ref=src, dst_ref=dst, send_sem=pair_send.at[i], recv_sem=pair_recv.at[i],
            device_id=(d, 1 - t), device_id_type=MESH,
        )

    corner_swap = swap(corner_out, corner_in, 2)
    corner_swap.start()
    landed(6)
    chosen = jnp.zeros((images, units_ref.shape[1]), F32)
    for q in range(GROUP):
        chosen += jnp.dot(back_in[q], onehot[q], preferred_element_type=F32)
    pick_ref[images + logits :] = chosen
    pick_out[...] = pick_ref[:, : 2 * panel]
    pick_swap = swap(pick_out, pick_in, 1)
    pick_swap.start()
    corner_swap.wait()
    pick_swap.wait()
    top_ref[...] = jnp.where(t == 0, pick_out[...], pick_in[...])
    corner_ref[...] = jnp.where(
        t == 0, corner_out[...].astype(F32), corner_in[...].astype(F32)
    ).astype(BF16)
    for copy in sent:
        copy.wait_send()
    for w, buf in enumerate((wu, wd, pan)):
        for s in range(planes):
            @pl.when((z >= s) & (z < last))
            def _():
                hop(buf, w, z - s, s, 1).wait_send()

            @pl.when((z + s <= last) & (z > 0))
            def _():
                hop(buf, w, z + s, s, -1).wait_send()


def fused_front(normed, residual_in, w_up, w_down, gain, head, inputs, units, panels, members):
    images, width = normed.shape
    depth, hidden_dev = w_up.shape
    logits = head.shape[0]
    panel = panels.shape[1] * members
    rows_dev = units.shape[1]
    planes = members // GROUP
    cols = hidden_dev // GROUP
    side = images + logits
    total = side + images
    dma = pltpu.SemaphoreType.DMA
    vmem = pl.BlockSpec(memory_space=pltpu.VMEM)
    hbm = pl.BlockSpec(memory_space=pltpu.HBM)
    return pl.pallas_call(
        functools.partial(front_kernel, planes, panel),
        out_shape=(
            jax.ShapeDtypeStruct((total, rows_dev), F32),
            jax.ShapeDtypeStruct((total, 2 * panel), F32),
            jax.ShapeDtypeStruct((images, logits), F32),
            jax.ShapeDtypeStruct((2, panel, rows_dev), BF16),
            jax.ShapeDtypeStruct((panel, panel), BF16),
        ),
        in_specs=[hbm] * 4 + [vmem] * 4 + [hbm],
        out_specs=(vmem,) * 5,
        scratch_shapes=[
            pltpu.VMEM((images, width), BF16),
            pltpu.VMEM((images, width), BF16),
            pltpu.VMEM((GROUP, images, width), BF16),
            pltpu.VMEM((planes, GROUP, depth, cols), BF16),
            pltpu.VMEM((planes, GROUP, depth, cols), BF16),
            pltpu.VMEM((GROUP, images, width), BF16),
            pltpu.VMEM((GROUP - 1, images, width), BF16),
            pltpu.VMEM((GROUP, images, width), F32),
            pltpu.VMEM((images, width), F32),
            pltpu.VMEM((images, width), BF16),
            pltpu.VMEM((GROUP, images, width), BF16),
            pltpu.VMEM((GROUP, images, cols), F32),
            pltpu.VMEM((GROUP, images, cols), F32),
            pltpu.VMEM((logits, cols), F32),
            pltpu.VMEM((GROUP, logits, cols), F32),
            pltpu.VMEM((GROUP, images, cols), BF16),
            pltpu.VMEM((GROUP, images, cols), BF16),
            pltpu.VMEM((GROUP, cols, rows_dev), BF16),
            pltpu.VMEM((images, width), F32),
            pltpu.VMEM((total, 2 * panel), F32),
            pltpu.VMEM((total, 2 * panel), F32),
            pltpu.VMEM((planes, GROUP) + panels.shape, BF16),
            pltpu.VMEM((panel, panel), BF16),
            pltpu.VMEM((panel, panel), BF16),
            dma((5,)),
            dma((9, GROUP)),
            dma((9, GROUP)),
            dma((3, planes)),
            dma((3, planes)),
            dma((3, planes)),
            dma((3, planes)),
            dma((3,)),
            dma((3,)),
        ],
        compiler_params=pltpu.CompilerParams(
            collective_id=0, has_side_effects=True, vmem_limit_bytes=60 * 1024 * 1024
        ),
        cost_estimate=pl.CostEstimate(
            flops=16 * images * width * hidden_dev,
            bytes_accessed=800 * depth * hidden_dev,
            transcendentals=2 * images * hidden_dev,
        ),
    )(normed, residual_in, w_up, w_down.T, gain, head, inputs, units, panels)


def tail_kernel(
    panel, gain_ref, bent_ref, head_ref, top_gain_ref, top_bent_ref, top_head_ref, project_ref,
    panels_ref, corner_ref, inverses_ref, out_ref,
):
    t = lax.axis_index("tensor")
    images, rows_dev = gain_ref.shape
    logits = head_ref.shape[0]
    project = project_ref[...].reshape(images, logits, 1)

    def jacobian(gain, head, bent):
        value = gain[:, None, :] * (head[None, :, :] - project * bent[:, None, :])
        return value.reshape(images * logits, gain.shape[1]).astype(BF16)

    def solve(block, inverse):
        return lax.dot_general(
            block, inverse, (((1,), (1,)), ((), ())), preferred_element_type=F32
        ).astype(BF16)

    top = jacobian(top_gain_ref[...], top_head_ref[...], top_bent_ref[...])
    first = solve(top[:, :panel], inverses_ref[0])
    second_in = top[:, panel:].astype(F32) - jnp.dot(
        first, corner_ref[...], preferred_element_type=F32
    )
    second = solve(second_in.astype(BF16), inverses_ref[1])
    solved = jnp.concatenate([first, second], axis=1)
    lower = panels_ref[...].reshape(2 * panel, rows_dev)
    update = jnp.dot(solved, lower, preferred_element_type=F32)
    jac = jacobian(gain_ref[...], head_ref[...], bent_ref[...])
    below = jac.astype(F32) - update
    out_ref[:, 2 * panel :] = below[:, 2 * panel :].astype(BF16)
    out_ref[:, : 2 * panel] = jnp.where(
        t == 0, solved.astype(F32), below[:, : 2 * panel]
    ).astype(BF16)


def tail(pick, top, project, gathered, corner, inverses, images, logits):
    panel = inverses.shape[1]
    rows_dev = pick.shape[1]
    step = 16 if images % 16 == 0 else images

    def rows(count, columns):
        return pl.BlockSpec((count, columns), lambda i: (i, 0))

    def whole(*shape):
        return pl.BlockSpec(shape, lambda i: (0,) * len(shape))

    def cut(values):
        return values[:images], values[images + logits :], values[images : images + logits]

    return pl.pallas_call(
        functools.partial(tail_kernel, panel),
        grid=(images // step,),
        out_shape=jax.ShapeDtypeStruct((images * logits, rows_dev), BF16),
        in_specs=[
            rows(step, rows_dev), rows(step, rows_dev), whole(logits, rows_dev),
            rows(step, 2 * panel), rows(step, 2 * panel), whole(logits, 2 * panel),
            rows(step * logits, 1),
            whole(2, panel, rows_dev), whole(panel, panel), whole(2, panel, panel),
        ],
        out_specs=rows(step * logits, rows_dev),
        compiler_params=pltpu.CompilerParams(vmem_limit_bytes=40 * 1024 * 1024),
    )(
        *cut(pick), *cut(top), project.reshape(images * logits, 1), gathered, corner, inverses
    )


def plain_front(normed, residual_in, w_up, w_down, head_pair):
    images = normed.shape[0]
    logits = head_pair.shape[0] // 2
    up_pre = jnp.dot(
        normed, lax.all_gather(w_up, "dp", axis=0, tiled=True), preferred_element_type=F32
    )
    activ, slope = gelu_parts(up_pre)
    down_full = lax.all_gather(w_down, "dp", axis=1, tiled=True)
    partial_out = jnp.dot(activ.astype(BF16), down_full, preferred_element_type=F32)
    block_out = residual_in.astype(F32) + lax.psum(partial_out, "tensor")
    xhat, inv_std = normalize(block_out)
    both = jnp.concatenate([head_pair, xhat.astype(BF16)], axis=0)
    out = lax.dot_general(both, down_full, (((1,), (1,)), ((), ())), preferred_element_type=F32)
    head_back = out[:logits] + out[logits : 2 * logits]
    return jnp.concatenate([slope, head_back], axis=0), out[2 * logits :], xhat, inv_std


def from_first(value, tensor_rank):
    return lax.psum(jnp.where(tensor_rank == 0, value, jnp.zeros_like(value)), "tensor")


def body(
    members,
    ranks,
    normed,
    residual_in,
    w_up,
    w_down,
    final_gain,
    head_cols,
    sub_inputs,
    sub_hidden,
    panels,
    inverses,
):
    images, width = normed.shape
    hidden_dev = w_up.shape[1]
    logits = head_cols.shape[1]
    panel = inverses.shape[1]
    rows_dev = sub_inputs.shape[0]
    tensor_rank = lax.axis_index("tensor")

    local_hidden = sub_hidden - tensor_rank * hidden_dev

    fits = (
        ranks == 2
        and members % GROUP == 0
        and hidden_dev % (GROUP * 128) == 0
        and w_up.shape[0] % 16 == 0
        and images % 16 == 0
        and panels.shape[1] % 16 == 0
        and members >= 3 * GROUP
    )
    if fits:
        pick, top, project, gathered, corner = fused_front(
            normed, residual_in, w_up, w_down, final_gain[None, :], head_cols.T,
            sub_inputs[None, :], local_hidden[None, :], panels, members,
        )
    else:
        gathered = lax.all_gather(panels, "dp", axis=1, tiled=True)
        corner = from_first(gathered[0, :, panel : 2 * panel], tensor_rank)
        scaled_head = (final_gain[:, None] * head_cols.astype(F32)).T
        centred_head = scaled_head - jnp.mean(scaled_head, axis=1, keepdims=True)
        head_pair = jnp.concatenate(halves(centred_head), axis=0)
        side, back, xhat, inv_std = plain_front(normed, residual_in, w_up, w_down, head_pair)
        project = lax.dot_general(
            xhat, centred_head, (((1,), (1,)), ((), ())), precision=lax.Precision.HIGHEST
        ) / width
        picked = jnp.take(normed, sub_inputs, axis=1).astype(F32)
        chosen = jnp.take(jnp.concatenate([side, back], axis=0), local_hidden, axis=1)
        pick = jnp.concatenate([chosen[:images] * picked * inv_std, chosen[images:]], axis=0)
        top = from_first(pick[:, : 2 * panel], tensor_rank)
    result = tail(pick, top, project, gathered, corner, inverses, images, logits)
    return result.reshape(images, logits, rows_dev)


def solution(mesh):
    in_specs = (
        P("dp", None),
        P("dp", None),
        P("dp", "tensor"),
        P("tensor", "dp"),
        P(),
        P(),
        P("tensor"),
        P("tensor"),
        P(None, "dp", "tensor"),
        P(),
    )
    out_specs = P("dp", None, "tensor")
    return jax.shard_map(
        functools.partial(body, mesh.shape["dp"], mesh.shape["tensor"]),
        mesh=mesh, in_specs=in_specs, out_specs=out_specs, check_vma=False,
    )
```

```python
import functools

import jax
import jax.numpy as jnp
from jax import lax
from jax.experimental import pallas as pl
from jax.experimental.pallas import tpu as pltpu
from jax.sharding import PartitionSpec as P

MESH = pl.DeviceIdType.MESH
GROUP = 4
F32 = jnp.float32
BF16 = jnp.bfloat16


def gelu_parts(values):
    normal_cdf = 0.5 * (1.0 + lax.erf(values * 0.7071067811865476))
    slope = normal_cdf + values * jnp.exp(-0.5 * values * values) * 0.3989422804014327
    return (values * normal_cdf, slope)


def normalize(block_result):
    mean_x = jnp.mean(block_result, axis=1, keepdims=True)
    centred = block_result - mean_x
    inv_std = lax.rsqrt(jnp.mean(centred * centred, axis=1, keepdims=True) + 1e-06)
    return centred * inv_std, inv_std


def halves(values):
    high = values.astype(BF16)
    return high, (values - high.astype(F32)).astype(BF16)


def pick_columns(values, index, size):
    where = lax.broadcasted_iota(jnp.int32, (size, index.shape[1]), 0)
    chosen = jnp.where(where == index, 1.0, 0.0).astype(BF16)
    return jnp.dot(values, chosen, preferred_element_type=F32)


def front_kernel(
    planes,
    panel,
    normed_hbm, resid_hbm, wup_ref, wdt_ref, gain_ref, head_ref, inputs_ref, units_ref, panels_hbm,
    pick_ref, top_ref, project_ref, panels_ref, corner_ref,
    normed_ref, resid_ref, nall, wu, wd, part, parts_in, pair_out, pair_in, xown, xall,
    slope_src, slope_in, head_src, head_in, back_src, back_in, onehot, xsum, pick_out, pick_in,
    pan, corner_out, corner_in,
    local_sem, flat_send, flat_recv, up_send, up_recv, dn_send, dn_recv, pair_send, pair_recv,
):
    d = lax.axis_index("dp")
    t = lax.axis_index("tensor")
    z = d // GROUP
    p = lax.rem(d, GROUP)
    images, width = normed_ref.shape
    cols = wu.shape[3]
    logits = head_ref.shape[0]
    last = planes - 1
    others = range(1, GROUP)

    barrier = pltpu.get_barrier_semaphore()
    for o in others:
        pl.semaphore_signal(barrier, inc=1, device_id=(z * GROUP + (p ^ o), t), device_id_type=MESH)
    pl.semaphore_signal(barrier, inc=1, device_id=(d, 1 - t), device_id_type=MESH)

    @pl.when(z > 0)
    def _():
        pl.semaphore_signal(barrier, inc=1, device_id=(d - GROUP, t), device_id_type=MESH)

    @pl.when(z < last)
    def _():
        pl.semaphore_signal(barrier, inc=1, device_id=(d + GROUP, t), device_id_type=MESH)

    pl.semaphore_wait(barrier, GROUP + jnp.where(z > 0, 1, 0) + jnp.where(z < last, 1, 0))

    def flat(src, dst, kind, o):
        return pltpu.make_async_remote_copy(
            src_ref=src, dst_ref=dst, send_sem=flat_send.at[kind, o], recv_sem=flat_recv.at[kind, o],
            device_id=(z * GROUP + (p ^ o), t), device_id_type=MESH,
        )

    def block(ref, q):
        return ref.at[:, pl.ds(pl.multiple_of(q * cols, 128), cols)]

    sent = []
    own = [
        pltpu.make_async_copy(block(wup_ref, p), wu.at[z, p], local_sem.at[0]),
        pltpu.make_async_copy(block(wdt_ref, p), wd.at[z, p], local_sem.at[1]),
        pltpu.make_async_copy(normed_hbm, normed_ref, local_sem.at[2]),
        pltpu.make_async_copy(resid_hbm, resid_ref, local_sem.at[3]),
        pltpu.make_async_copy(panels_hbm, pan.at[z, p], local_sem.at[4]),
    ]
    moves = {}

    def spread(kind, pick, dst):
        for o in others:
            copy = flat(pick(p ^ o), dst, kind, o)
            copy.start()
            moves[kind, o] = copy
            sent.append(copy)

    def landed(kind):
        for o in others:
            moves[kind, o].wait_recv()

    spread(0, lambda q: block(wup_ref, q), wu.at[z, p])
    for copy in own:
        copy.start()
    def selected(parts):
        chosen = 0.0
        for q in range(GROUP):
            both = jnp.concatenate(halves(parts[q]), axis=0)
            chosen += jnp.dot(both, onehot[q], preferred_element_type=F32)
        count = parts.shape[1]
        return chosen[:count] + chosen[count:]

    def hop(buf, w, src, s, step):
        send, recv = (up_send, up_recv) if step > 0 else (dn_send, dn_recv)
        return pltpu.make_async_remote_copy(
            src_ref=buf.at[src], dst_ref=buf.at[src], send_sem=send.at[w, s], recv_sem=recv.at[w, s],
            device_id=(d + step * GROUP, t), device_id_type=MESH,
        )

    def chunk_out(buf, w, q):
        def send(step, sems, marks):
            pltpu.make_async_remote_copy(
                src_ref=buf.at[z, q], dst_ref=buf.at[z, q], send_sem=sems.at[w, 0],
                recv_sem=marks.at[w, 0], device_id=(d + step * GROUP, t), device_id_type=MESH,
            ).start()

        @pl.when(z < last)
        def _():
            send(1, up_send, up_recv)

        @pl.when(z > 0)
        def _():
            send(-1, dn_send, dn_recv)

    def relay(buf, w, s):
        @pl.when(z >= s)
        def _():
            if s > 0:
                hop(buf, w, z - s, s - 1, 1).wait_recv()

            @pl.when(z < last)
            def _():
                hop(buf, w, z - s, s, 1).start()

        @pl.when(z + s <= last)
        def _():
            if s > 0:
                hop(buf, w, z + s, s - 1, -1).wait_recv()

            @pl.when(z > 0)
            def _():
                hop(buf, w, z + s, s, -1).start()

    own[0].wait()
    chunk_out(wu, 0, p)
    for o in others:
        moves[0, o].wait_recv()
        chunk_out(wu, 0, p ^ o)
    spread(1, lambda q: block(wdt_ref, q), wd.at[z, p])
    own[1].wait()
    chunk_out(wd, 1, p)
    for o in others:
        moves[1, o].wait_recv()
        chunk_out(wd, 1, p ^ o)
    own[2].wait()
    own[3].wait()
    nall[p] = normed_ref[...]
    head = head_ref[...].astype(F32) * gain_ref[...]
    head = head - jnp.mean(head, axis=1, keepdims=True)
    head_high, head_low = halves(head)
    head_pair = jnp.concatenate([head_high, head_low], axis=0)
    spread(2, lambda q: normed_ref, nall.at[p])
    spread(7, lambda q: panels_hbm, pan.at[z, p])
    own[4].wait()
    picked = pick_columns(normed_ref[...], inputs_ref[...], width)
    chunk = lax.broadcasted_iota(jnp.int32, (cols, units_ref.shape[1]), 0)
    relay(wu, 0, 1)
    for q in range(GROUP):
        onehot[q] = jnp.where(chunk + (t * GROUP + q) * cols == units_ref[...], 1.0, 0.0).astype(BF16)
    landed(2)
    for s in range(2, planes):
        relay(wu, 0, s)
        if s == 2:
            relay(wd, 1, 1)

    rows = GROUP * images
    up_pre = jnp.dot(
        nall[...].reshape(rows, width), wu[...].reshape(width, cols), preferred_element_type=F32
    )
    activ, slope = gelu_parts(up_pre)
    hidden = activ.astype(BF16)
    slope_src[...] = slope.reshape(GROUP, images, cols)
    spread(5, lambda q: slope_src.at[q], slope_in.at[p])
    slope_in[p] = slope_src[p]
    for s in range(2, planes - 1):
        relay(wd, 1, s)
    landed(5)
    pick_ref[:images] = selected(slope_in) * picked
    landed(7)
    relay(wd, 1, planes - 1)
    relay(pan, 2, 0)
    down = wd[...].reshape(width, cols)
    partial = lax.dot_general(hidden, down, (((1,), (1,)), ((), ())), preferred_element_type=F32)
    pair_out[...] = partial.reshape(GROUP, images, width)
    part[...] = partial.astype(BF16).reshape(GROUP, images, width)
    for o in others:
        copy = flat(part.at[p ^ o], parts_in.at[o - 1], 3, o)
        copy.start()
        moves[3, o] = copy
        sent.append(copy)
    head_back = jnp.dot(head_pair, down, preferred_element_type=F32)
    head_back = head_back[:logits] + head_back[logits:]
    head_src[...] = head_back
    spread(8, lambda q: head_src, head_in.at[p])
    head_in[p] = head_back
    total = pair_out[p]
    for o in others:
        moves[3, o].wait_recv()
        total = total + parts_in[o - 1].astype(F32)
    xsum[...] = total
    swap = pltpu.make_async_remote_copy(
        src_ref=xsum, dst_ref=pair_in, send_sem=pair_send.at[0], recv_sem=pair_recv.at[0],
        device_id=(d, 1 - t), device_id_type=MESH,
    )
    swap.start()
    swap.wait()
    block_out = resid_ref[...].astype(F32) + (xsum[...] + pair_in[...])
    xhat, inv_std = normalize(block_out)
    xown[...] = xhat.astype(BF16)
    spread(4, lambda q: xown, xall.at[p])
    relay(pan, 2, 1)
    xall[p] = xown[...]
    x_high, x_low = halves(xhat)
    nums = (((1,), (1,)), ((), ()))
    project = lax.dot_general(x_high, head_high, nums, preferred_element_type=F32)
    project += lax.dot_general(x_low, head_high, nums, preferred_element_type=F32)
    project += lax.dot_general(x_high, head_low, nums, preferred_element_type=F32)
    project_ref[...] = project * (1.0 / width)
    landed(4)
    back = jnp.dot(xall[...].reshape(rows, width), down, preferred_element_type=F32)
    back_src[...] = back.astype(BF16).reshape(GROUP, images, cols)
    spread(6, lambda q: back_src.at[q], back_in.at[p])
    back_in[p] = back_src[p]
    landed(8)
    pick_ref[:images] = pick_ref[:images] * inv_std
    pick_ref[images : images + logits] = selected(head_in)
    for s in range(2, planes):
        relay(pan, 2, s)
    for q in range(2):
        panels_ref[q] = pan[:, :, q].reshape(panels_ref.shape[1:])
    corner_out[...] = panels_ref[0, :, panel : 2 * panel]

    def swap(src, dst, i):
        return pltpu.make_async_remote_copy(
            src_ref=src, dst_ref=dst, send_sem=pair_send.at[i], recv_sem=pair_recv.at[i],
            device_id=(d, 1 - t), device_id_type=MESH,
        )

    corner_swap = swap(corner_out, corner_in, 2)
    corner_swap.start()
    landed(6)
    chosen = jnp.zeros((images, units_ref.shape[1]), F32)
    for q in range(GROUP):
        chosen += jnp.dot(back_in[q], onehot[q], preferred_element_type=F32)
    pick_ref[images + logits :] = chosen
    pick_out[...] = pick_ref[:, : 2 * panel]
    pick_swap = swap(pick_out, pick_in, 1)
    pick_swap.start()
    corner_swap.wait()
    pick_swap.wait()
    top_ref[...] = jnp.where(t == 0, pick_out[...], pick_in[...])
    corner_ref[...] = jnp.where(
        t == 0, corner_out[...].astype(F32), corner_in[...].astype(F32)
    ).astype(BF16)
    for copy in sent:
        copy.wait_send()
    for w, buf in enumerate((wu, wd, pan)):
        for s in range(planes):
            @pl.when((z >= s) & (z < last))
            def _():
                hop(buf, w, z - s, s, 1).wait_send()

            @pl.when((z + s <= last) & (z > 0))
            def _():
                hop(buf, w, z + s, s, -1).wait_send()


def fused_front(normed, residual_in, w_up, w_down, gain, head, inputs, units, panels, members):
    images, width = normed.shape
    depth, hidden_dev = w_up.shape
    logits = head.shape[0]
    panel = panels.shape[1] * members
    rows_dev = units.shape[1]
    planes = members // GROUP
    cols = hidden_dev // GROUP
    side = images + logits
    total = side + images
    dma = pltpu.SemaphoreType.DMA
    vmem = pl.BlockSpec(memory_space=pltpu.VMEM)
    hbm = pl.BlockSpec(memory_space=pltpu.HBM)
    return pl.pallas_call(
        functools.partial(front_kernel, planes, panel),
        out_shape=(
            jax.ShapeDtypeStruct((total, rows_dev), F32),
            jax.ShapeDtypeStruct((total, 2 * panel), F32),
            jax.ShapeDtypeStruct((images, logits), F32),
            jax.ShapeDtypeStruct((2, panel, rows_dev), BF16),
            jax.ShapeDtypeStruct((panel, panel), BF16),
        ),
        in_specs=[hbm] * 4 + [vmem] * 4 + [hbm],
        out_specs=(vmem,) * 5,
        scratch_shapes=[
            pltpu.VMEM((images, width), BF16),
            pltpu.VMEM((images, width), BF16),
            pltpu.VMEM((GROUP, images, width), BF16),
            pltpu.VMEM((planes, GROUP, depth, cols), BF16),
            pltpu.VMEM((planes, GROUP, depth, cols), BF16),
            pltpu.VMEM((GROUP, images, width), BF16),
            pltpu.VMEM((GROUP - 1, images, width), BF16),
            pltpu.VMEM((GROUP, images, width), F32),
            pltpu.VMEM((images, width), F32),
            pltpu.VMEM((images, width), BF16),
            pltpu.VMEM((GROUP, images, width), BF16),
            pltpu.VMEM((GROUP, images, cols), F32),
            pltpu.VMEM((GROUP, images, cols), F32),
            pltpu.VMEM((logits, cols), F32),
            pltpu.VMEM((GROUP, logits, cols), F32),
            pltpu.VMEM((GROUP, images, cols), BF16),
            pltpu.VMEM((GROUP, images, cols), BF16),
            pltpu.VMEM((GROUP, cols, rows_dev), BF16),
            pltpu.VMEM((images, width), F32),
            pltpu.VMEM((total, 2 * panel), F32),
            pltpu.VMEM((total, 2 * panel), F32),
            pltpu.VMEM((planes, GROUP) + panels.shape, BF16),
            pltpu.VMEM((panel, panel), BF16),
            pltpu.VMEM((panel, panel), BF16),
            dma((5,)),
            dma((9, GROUP)),
            dma((9, GROUP)),
            dma((3, planes)),
            dma((3, planes)),
            dma((3, planes)),
            dma((3, planes)),
            dma((3,)),
            dma((3,)),
        ],
        compiler_params=pltpu.CompilerParams(
            collective_id=0, has_side_effects=True, vmem_limit_bytes=60 * 1024 * 1024
        ),
        cost_estimate=pl.CostEstimate(
            flops=16 * images * width * hidden_dev,
            bytes_accessed=800 * depth * hidden_dev,
            transcendentals=2 * images * hidden_dev,
        ),
    )(normed, residual_in, w_up, w_down.T, gain, head, inputs, units, panels)


def tail_kernel(
    panel, gain_ref, bent_ref, head_ref, top_gain_ref, top_bent_ref, top_head_ref, project_ref,
    panels_ref, corner_ref, inverses_ref, out_ref,
):
    t = lax.axis_index("tensor")
    images, rows_dev = gain_ref.shape
    logits = head_ref.shape[0]
    project = project_ref[...].reshape(images, logits, 1)

    def jacobian(gain, head, bent):
        value = gain[:, None, :] * (head[None, :, :] - project * bent[:, None, :])
        return value.reshape(images * logits, gain.shape[1]).astype(BF16)

    def solve(block, inverse):
        return lax.dot_general(
            block, inverse, (((1,), (1,)), ((), ())), preferred_element_type=F32
        ).astype(BF16)

    top = jacobian(top_gain_ref[...], top_head_ref[...], top_bent_ref[...])
    first = solve(top[:, :panel], inverses_ref[0])
    second_in = top[:, panel:].astype(F32) - jnp.dot(
        first, corner_ref[...], preferred_element_type=F32
    )
    second = solve(second_in.astype(BF16), inverses_ref[1])
    solved = jnp.concatenate([first, second], axis=1)
    lower = panels_ref[...].reshape(2 * panel, rows_dev)
    update = jnp.dot(solved, lower, preferred_element_type=F32)
    jac = jacobian(gain_ref[...], head_ref[...], bent_ref[...])
    below = jac.astype(F32) - update
    out_ref[:, 2 * panel :] = below[:, 2 * panel :].astype(BF16)
    out_ref[:, : 2 * panel] = jnp.where(
        t == 0, solved.astype(F32), below[:, : 2 * panel]
    ).astype(BF16)


def tail(pick, top, project, gathered, corner, inverses, images, logits):
    panel = inverses.shape[1]
    rows_dev = pick.shape[1]
    step = logits
    last = images // step

    def rows(count, columns):
        return pl.BlockSpec((count, columns), lambda i: (i, 0))

    def whole(*shape):
        return pl.BlockSpec(shape, lambda i: (0,) * len(shape))

    def parts(columns):
        return [
            pl.BlockSpec((step, columns), lambda i: (i, 0)),
            pl.BlockSpec((step, columns), lambda i: (last + 1 + i, 0)),
            pl.BlockSpec((step, columns), lambda i: (last, 0)),
        ]

    return pl.pallas_call(
        functools.partial(tail_kernel, panel),
        grid=(images // step,),
        out_shape=jax.ShapeDtypeStruct((images * logits, rows_dev), BF16),
        in_specs=[
            *parts(rows_dev),
            *parts(2 * panel),
            rows(step * logits, 1),
            whole(2, panel, rows_dev), whole(panel, panel), whole(2, panel, panel),
        ],
        out_specs=rows(step * logits, rows_dev),
        compiler_params=pltpu.CompilerParams(vmem_limit_bytes=40 * 1024 * 1024),
    )(
        pick, pick, pick, top, top, top, project.reshape(images * logits, 1), gathered, corner, inverses
    )


def plain_front(normed, residual_in, w_up, w_down, head_pair):
    images = normed.shape[0]
    logits = head_pair.shape[0] // 2
    up_pre = jnp.dot(
        normed, lax.all_gather(w_up, "dp", axis=0, tiled=True), preferred_element_type=F32
    )
    activ, slope = gelu_parts(up_pre)
    down_full = lax.all_gather(w_down, "dp", axis=1, tiled=True)
    partial_out = jnp.dot(activ.astype(BF16), down_full, preferred_element_type=F32)
    block_out = residual_in.astype(F32) + lax.psum(partial_out, "tensor")
    xhat, inv_std = normalize(block_out)
    both = jnp.concatenate([head_pair, xhat.astype(BF16)], axis=0)
    out = lax.dot_general(both, down_full, (((1,), (1,)), ((), ())), preferred_element_type=F32)
    head_back = out[:logits] + out[logits : 2 * logits]
    return jnp.concatenate([slope, head_back], axis=0), out[2 * logits :], xhat, inv_std


def from_first(value, tensor_rank):
    return lax.psum(jnp.where(tensor_rank == 0, value, jnp.zeros_like(value)), "tensor")


def body(
    members,
    ranks,
    normed,
    residual_in,
    w_up,
    w_down,
    final_gain,
    head_cols,
    sub_inputs,
    sub_hidden,
    panels,
    inverses,
):
    images, width = normed.shape
    hidden_dev = w_up.shape[1]
    logits = head_cols.shape[1]
    panel = inverses.shape[1]
    rows_dev = sub_inputs.shape[0]
    tensor_rank = lax.axis_index("tensor")

    local_hidden = sub_hidden - tensor_rank * hidden_dev

    fits = (
        ranks == 2
        and members % GROUP == 0
        and hidden_dev % (GROUP * 128) == 0
        and w_up.shape[0] % 16 == 0
        and images % 16 == 0
        and panels.shape[1] % 16 == 0
        and members >= 3 * GROUP
    )
    if fits:
        pick, top, project, gathered, corner = fused_front(
            normed, residual_in, w_up, w_down, final_gain[None, :], head_cols.T,
            sub_inputs[None, :], sub_hidden[None, :], panels, members,
        )
    else:
        gathered = lax.all_gather(panels, "dp", axis=1, tiled=True)
        corner = from_first(gathered[0, :, panel : 2 * panel], tensor_rank)
        scaled_head = (final_gain[:, None] * head_cols.astype(F32)).T
        centred_head = scaled_head - jnp.mean(scaled_head, axis=1, keepdims=True)
        head_pair = jnp.concatenate(halves(centred_head), axis=0)
        side, back, xhat, inv_std = plain_front(normed, residual_in, w_up, w_down, head_pair)
        project = lax.dot_general(
            xhat, centred_head, (((1,), (1,)), ((), ())), precision=lax.Precision.HIGHEST
        ) / width
        picked = jnp.take(normed, sub_inputs, axis=1).astype(F32)
        chosen = jnp.take(jnp.concatenate([side, back], axis=0), local_hidden, axis=1)
        pick = jnp.concatenate([chosen[:images] * picked * inv_std, chosen[images:]], axis=0)
        top = from_first(pick[:, : 2 * panel], tensor_rank)
    result = tail(pick, top, project, gathered, corner, inverses, images, logits)
    return result.reshape(images, logits, rows_dev)


def solution(mesh):
    in_specs = (
        P("dp", None),
        P("dp", None),
        P("dp", "tensor"),
        P("tensor", "dp"),
        P(),
        P(),
        P("tensor"),
        P("tensor"),
        P(None, "dp", "tensor"),
        P(),
    )
    out_specs = P("dp", None, "tensor")
    return jax.shard_map(
        functools.partial(body, mesh.shape["dp"], mesh.shape["tensor"]),
        mesh=mesh, in_specs=in_specs, out_specs=out_specs, check_vma=False,
    )
```
